512 devices in a mesh: row: 64 (over y, z), col: 8 (over x, core).
Axes of the slice: x: 4, y: 8, z: 8, core: 2. Of those that a mesh axis runs over, the one named last changes fastest.
Arguments:
- right_sides: float32 [8, 4096, 256], P(None, 'row'), may hold values from -6 to 6
- diag_inverse: float32 [4, 4096, 4096], P(None, 'col', 'row'), may hold values from -0.25 to 0.25
- lower_blocks: float32 [6, 4096, 4096], P(None, 'row', 'col'), may hold values from -0.046875 to 0.046875
- trail_panel: float32 [4, 4096, 4, 4096], P(None, 'row', None, 'col'), may hold values from -0.046875 to 0.046875
Outputs:
- solution: float32 [4, 4096, 256], P(None, 'col', 'row')
- trail_rest: float32 [4, 4096, 256], P(None, 'row', 'col')
The draws below stay inside these ranges and needn't reach their ends.
All inputs are finite; a program needn't handle non-finite values.
Results may differ from the reference program's by a relative error of at most 0.0001.
Values sent between devices are 32-bit elements; how exact they have to be, the bound alone decides.
No kernel may reach another device: no remote copies, remote signals or barrier semaphores. Data moves between devices by JAX's collectives and lax.ppermute only.
A program may use at most 64 MiB of HBM per device.

```python
import jax
import jax.numpy as jnp
from jax import lax

NB = 4096
R = 256
STEPS = 4
TB = 4
PAIRS = 6
MB = 8


def spiked(values, own_key, source, target, shards_of, factor):
    def block_of(position):
        return (jnp.arange(values.shape[position]) // (values.shape[position] // shards_of)).reshape((-1,) + (1,) * (values.ndim - 1 - position))

    one_side = jax.random.permutation(own_key, shards_of)[block_of(target)]
    far = (block_of(target) + shards_of // 2) % shards_of
    return jnp.where((block_of(source) == one_side) | (block_of(source) == far), factor * values, values)


def level_of(rng, extent, shards, least, high):
    def one(axis_at, blocks):
        steps = jax.random.uniform(jax.random.fold_in(jax.random.fold_in(rng, 6), axis_at), (blocks,), jnp.float32, least / len(shards), high / len(shards))
        return jnp.repeat(jnp.exp(steps), extent[axis_at] // blocks).reshape((-1,) + (1,) * (len(extent) - axis_at - 1))

    level = one(*shards[0])
    for cut in shards[1:]:
        level = level * one(*cut)
    return level


def bell_draw(stream_key, shape, deviation, bound, cuts=(), held_as=jnp.bfloat16):
    entries = deviation * jax.random.normal(stream_key, shape, jnp.float32)
    if cuts:
        entries = entries * level_of(stream_key, shape, cuts, -0.22, 0.18)
    return jnp.clip(entries, -bound, bound).astype(held_as)


def heavy_noise(key, extent, scale, limit, shards, heavy, dtype=jnp.bfloat16):
    values = scale * jax.random.normal(key, extent, jnp.float32)
    if shards:
        values = values * level_of(key, extent, shards, -0.22, 0.18)
    return jnp.clip(spiked(values, jax.random.fold_in(key, 3), *heavy), -limit, limit).astype(dtype)


def setup_inputs(seed: int = 0) -> dict:
    key_of = jax.random.split(jax.random.key(seed), 5)
    return {
        "right_sides": bell_draw(key_of[0], (MB, NB, R), 1.0, 6.0, ((1, 64),), jnp.float32),
        "diag_inverse": heavy_noise(key_of[1], (STEPS, NB, NB), NB ** -0.5, 0.25, ((1, 8), (2, 64)), (2, 1, 64, 4.0), jnp.float32),
        "lower_blocks": bell_draw(key_of[2], (PAIRS, NB, NB), (NB * STEPS) ** -0.5, 0.046875, ((1, 64), (2, 8)), jnp.float32),
        "trail_panel": bell_draw(key_of[3], (TB, NB, STEPS, NB), (NB * STEPS) ** -0.5, 0.046875, ((1, 64), (3, 8)), jnp.float32),
    }


HIGHEST_PREC = lax.Precision.HIGHEST


def pair_index(block_row, prior_row):
    return block_row * (block_row - 1) // 2 + prior_row


def reference(right_sides, diag_inverse, lower_blocks, trail_panel):
    solved = []
    for block_row in range(STEPS):
        current = right_sides[block_row]
        for prior_row in range(block_row):
            current = current - jnp.dot(lower_blocks[pair_index(block_row, prior_row)], solved[prior_row], precision=HIGHEST_PREC, preferred_element_type=jnp.float32)
        solved.append(jnp.dot(diag_inverse[block_row], current, precision=HIGHEST_PREC, preferred_element_type=jnp.float32))
    trail_rest = right_sides[STEPS:]
    for block_row in range(STEPS):
        trail_rest = trail_rest - jnp.einsum("mrn,nc->mrc", trail_panel[:, :, block_row, :], solved[block_row], precision=HIGHEST_PREC)
    return jnp.stack(solved), trail_rest
```

```python
import jax
import jax.numpy as jnp
from jax import lax
from jax.sharding import PartitionSpec as P

HIGHEST_PREC = lax.Precision.HIGHEST


def pair_index(block_row, prior_row):
    return block_row * (block_row - 1) // 2 + prior_row


def block_product(matrix, solved_block):
    return jnp.dot(matrix, solved_block, precision=HIGHEST_PREC, preferred_element_type=jnp.float32)


def reduce_scatter(value, axis):
    size = lax.axis_size(axis)
    pieces = lax.all_to_all(value, axis, 0, 0, tiled=True)
    return pieces.reshape((size, value.shape[0] // size) + value.shape[1:]).sum(0)


def replicate(piece, axis):
    size = lax.axis_size(axis)
    copies = jnp.broadcast_to(piece[None], (size,) + piece.shape)
    copies = copies.reshape((size * piece.shape[0],) + piece.shape[1:])
    return lax.all_to_all(copies, axis, 0, 0, tiled=True)


def sum_over(value, axis):
    size = lax.axis_size(axis)
    return replicate(value, axis).reshape((size,) + value.shape).sum(0)


def shards(right_sides, diag_inverse, lower_blocks, trail_panel):
    step_count = diag_inverse.shape[0]
    trail_count = trail_panel.shape[0]
    local_rows = right_sides.shape[1]
    column_count = right_sides.shape[2]
    solved = []
    pending = [None] * step_count
    trail_acc = None
    for block_row in range(step_count):
        if block_row == 0:
            current = right_sides[0]
        else:
            current = right_sides[block_row] - sum_over(pending[block_row], "col")
        local_term = block_product(diag_inverse[block_row], current)
        solved_block = replicate(reduce_scatter(local_term, "row"), "row")
        solved.append(solved_block)
        for later_row in range(block_row + 1, step_count):
            contrib = block_product(lower_blocks[pair_index(later_row, block_row)], solved_block)
            pending[later_row] = (
                contrib if pending[later_row] is None else pending[later_row] + contrib
            )
        contrib = jnp.einsum(
            "nc,mrn->cmr", solved_block, trail_panel[:, :, block_row, :], precision=HIGHEST_PREC
        )
        trail_acc = contrib if trail_acc is None else trail_acc + contrib
    shared = reduce_scatter(trail_acc.reshape(column_count, trail_count * local_rows), "col")
    own_width = shared.shape[0]
    shared = shared.reshape(own_width, trail_count, local_rows).transpose(1, 2, 0)
    own_sides = lax.dynamic_slice_in_dim(
        right_sides[step_count:], lax.axis_index("col") * own_width, own_width, 2
    )
    trail_rest = own_sides - shared
    stacked = jnp.stack(solved)
    out_width = column_count // lax.axis_size("row")
    solution = lax.dynamic_slice_in_dim(stacked, lax.axis_index("row") * out_width, out_width, 2)
    return (solution, trail_rest)


def solution(mesh):
    placed = (
        P(None, "row", None),
        P(None, "col", "row"),
        P(None, "row", "col"),
        P(None, "row", None, "col"),
    )
    return jax.shard_map(
        shards,
        mesh=mesh,
        in_specs=placed,
        out_specs=(P(None, "col", "row"), P(None, "row", "col")),
        check_vma=False,
    )
```

```python
import jax
import jax.numpy as jnp
from jax import lax
from jax.sharding import PartitionSpec as P

HIGHEST_PREC = lax.Precision.HIGHEST
GROUPS = 4
PART_ROWS = 8
PART_COLUMNS = 256


def pair_index(block_row, prior_row):
    return block_row * (block_row - 1) // 2 + prior_row


def times(left, right):
    return jnp.dot(left, right, precision=HIGHEST_PREC, preferred_element_type=jnp.float32)


def times_transposed(left, right):
    return lax.dot_general(
        left,
        right,
        (((1,), (1,)), ((), ())),
        precision=HIGHEST_PREC,
        preferred_element_type=jnp.float32,
    )


def to_parts(value):
    rows, columns = value.shape
    split = value.reshape(rows // PART_ROWS, PART_ROWS, columns // PART_COLUMNS, PART_COLUMNS)
    return split.transpose(0, 2, 1, 3).reshape(-1, PART_ROWS, PART_COLUMNS)


def from_parts(parts, columns):
    split = parts.reshape(-1, columns // PART_COLUMNS, PART_ROWS, PART_COLUMNS)
    return split.transpose(0, 2, 1, 3).reshape(-1, columns)


def swap(parts, axis, groups=None):
    return lax.all_to_all(parts, axis, 0, 0, axis_index_groups=groups, tiled=True)


def copies(part, count):
    return jnp.broadcast_to(part[None], (count,) + part.shape)


def sum_over(value, axis):
    return swap(copies(value, lax.axis_size(axis)), axis).sum(0)


def shards(right_sides, diag_inverse, lower_blocks, trail_panel):
    step_count = diag_inverse.shape[0]
    trail_count = trail_panel.shape[0]
    local_rows = right_sides.shape[1]
    column_count = right_sides.shape[2]
    row_size = lax.axis_size("row")
    col_size = lax.axis_size("col")
    members = row_size // GROUPS
    width = column_count // GROUPS
    row = lax.axis_index("row")
    group = row // members
    groups = [[g * members + m for m in range(members)] for g in range(GROUPS)]
    diag = diag_inverse.transpose(0, 2, 1)
    block_width = diag.shape[2]

    def from_partners(value):
        got = [value]
        for shift in range(1, GROUPS):
            pairs = [(r, (r - shift * members) % row_size) for r in range(row_size)]
            got.append(lax.ppermute(value, "row", pairs))
        return got

    def own_rows(value):
        return lax.dynamic_slice_in_dim(value, group * width, width, 0)

    later_sides = right_sides[1:step_count].reshape(-1, block_width)
    first = jnp.concatenate([lower_blocks[0], diag[1], later_sides], 0)
    second = jnp.concatenate(
        [lower_blocks[1:].reshape(-1, block_width), diag[2:].reshape(-1, block_width)], 0
    )
    first_all = from_partners(first)
    second_all = from_partners(second)

    def block_of(index, is_diag):
        if is_diag:
            source, at = (first_all, 1) if index == 1 else (second_all, 5 + index - 2)
        else:
            source, at = (first_all, 0) if index == 0 else (second_all, index - 1)
        return jnp.concatenate([s[at * local_rows : (at + 1) * local_rows] for s in source], 0)

    def sides_of(block_row):
        parts = []
        for s in first_all:
            sides = s[2 * local_rows :].reshape(step_count - 1, local_rows, column_count)
            parts.append(sides[block_row - 1])
        return own_rows(jnp.concatenate(parts, 0).T)

    trail = [
        trail_panel[:, :, j, :].reshape(trail_count * local_rows, block_width)
        for j in range(step_count)
    ]
    out_width = column_count // row_size
    outs = []
    grouped = []

    partial_value = times(right_sides[0].T, diag[0])
    part = swap(to_parts(partial_value), "row").sum(0)
    whole = from_parts(swap(copies(part, row_size), "row"), block_width)
    outs.append(lax.dynamic_slice_in_dim(whole, row * out_width, out_width, 0))
    trail_acc = times_transposed(whole, trail[0])
    grouped.append(own_rows(whole))

    for block_row in range(1, step_count):
        update = None
        for prior_row in range(block_row):
            block = block_of(pair_index(block_row, prior_row), False)
            term = times_transposed(grouped[prior_row], block)
            update = term if update is None else update + term
        current = sides_of(block_row) - sum_over(update, "col")
        partial_value = times(current, block_of(block_row, True))
        part = swap(to_parts(partial_value), "row", groups).sum(0)
        if block_row < step_count - 1:
            solved = from_parts(swap(copies(part, members), "row", groups), block_width)
            grouped.append(solved)
            place = (row % members) * out_width
            outs.append(lax.dynamic_slice_in_dim(solved, place, out_width, 0))
        else:
            whole = from_parts(swap(copies(part, row_size), "row"), block_width)
            outs.append(lax.dynamic_slice_in_dim(whole, row * out_width, out_width, 0))

    middle = jnp.stack(grouped[1:])
    spread = jnp.concatenate(from_partners(middle) * 2, 1)
    middle = lax.dynamic_slice_in_dim(spread, (GROUPS - group) % GROUPS * width, column_count, 1)
    for j in range(1, step_count - 1):
        trail_acc = trail_acc + times_transposed(middle[j - 1], trail[j])
    trail_acc = trail_acc + times_transposed(whole, trail[step_count - 1])

    own_width = column_count // col_size
    shared = swap(trail_acc.reshape(col_size, own_width, -1), "col").sum(0)
    shared = shared.reshape(own_width, trail_count, local_rows).transpose(1, 2, 0)
    own_sides = lax.dynamic_slice_in_dim(
        right_sides[step_count:], lax.axis_index("col") * own_width, own_width, 2
    )
    trail_rest = own_sides - shared
    return (jnp.stack(outs).transpose(0, 2, 1), trail_rest)


def solution(mesh):
    placed = (
        P(None, "row", None),
        P(None, "col", "row"),
        P(None, "row", "col"),
        P(None, "row", None, "col"),
    )
    return jax.shard_map(
        shards,
        mesh=mesh,
        in_specs=placed,
        out_specs=(P(None, "col", "row"), P(None, "row", "col")),
        check_vma=False,
    )
```

```python
import jax
import jax.numpy as jnp
from jax import lax
from jax.sharding import PartitionSpec as P

HIGHEST_PREC = lax.Precision.HIGHEST
Z_SIZE = 8


def pair_index(block_row, prior_row):
    return block_row * (block_row - 1) // 2 + prior_row


def times(left, right):
    return jnp.dot(left, right, precision=HIGHEST_PREC, preferred_element_type=jnp.float32)


def swap(parts, axis, groups=None):
    return lax.all_to_all(parts, axis, 0, 0, axis_index_groups=groups, tiled=True)


def copies(part, count):
    return jnp.broadcast_to(part[None], (count,) + part.shape)


def reduce_scatter(value, axis, count, groups=None):
    parts = value.reshape((count, value.shape[0] // count) + value.shape[1:])
    return swap(parts, axis, groups).sum(0)


def replicate(part, axis, count, groups=None):
    parts = swap(copies(part, count), axis, groups)
    return parts.reshape((-1,) + part.shape[1:])


def shards(right_sides, diag_inverse, lower_blocks, trail_panel):
    step_count = diag_inverse.shape[0]
    trail_count = trail_panel.shape[0]
    local_rows = right_sides.shape[1]
    column_count = right_sides.shape[2]
    row_size = lax.axis_size("row")
    col_size = lax.axis_size("col")
    members = row_size // 2
    half = column_count // 2
    row = lax.axis_index("row")
    group = row // Z_SIZE % 2
    groups = [[r for r in range(row_size) if r // Z_SIZE % 2 == g] for g in range(2)]
    partners = [(r, r + Z_SIZE if r // Z_SIZE % 2 == 0 else r - Z_SIZE) for r in range(row_size)]

    def from_partner(value):
        return lax.ppermute(value, "row", partners)

    def half_of(value, which):
        return lax.dynamic_slice_in_dim(value, which * half, half, value.ndim - 1)

    own_diag = diag_inverse.transpose(0, 2, 1)
    later_sides = right_sides[1:step_count]
    got_sides = from_partner(half_of(later_sides, 1 - group))
    first = from_partner(jnp.stack([lower_blocks[0], own_diag[1]]))
    second = from_partner(jnp.concatenate([lower_blocks[1:], own_diag[2:]]))
    got_lower = [first[0]] + [second[i] for i in range(lower_blocks.shape[0] - 1)]
    got_diag = [None, first[1]] + [
        second[lower_blocks.shape[0] - 1 + i] for i in range(step_count - 2)
    ]
    own_sides_half = half_of(later_sides, group)

    part = reduce_scatter(times(diag_inverse[0], right_sides[0]), "row", row_size)
    whole = replicate(part, "row", row_size)
    solved = [whole]
    halves = [half_of(whole, group)]

    for block_row in range(1, step_count):
        update = None
        for prior_row in range(block_row):
            index = pair_index(block_row, prior_row)
            term = jnp.stack(
                [
                    times(lower_blocks[index], halves[prior_row]),
                    times(got_lower[index], halves[prior_row]),
                ]
            )
            update = term if update is None else update + term
        total = swap(copies(update, col_size), "col").sum(0)
        current = own_sides_half[block_row - 1] - total[0]
        partner_current = got_sides[block_row - 1] - total[1]
        partial_value = times(diag_inverse[block_row], current) + times(
            got_diag[block_row].T, partner_current
        )
        part = reduce_scatter(partial_value, "row", members, groups)
        if block_row < step_count - 1:
            solved_half = replicate(part, "row", members, groups)
            halves.append(solved_half)
            other = from_partner(solved_half)
            solved.append(
                jnp.concatenate(
                    [
                        jnp.where(group == 0, solved_half, other),
                        jnp.where(group == 0, other, solved_half),
                    ],
                    1,
                )
            )
        else:
            parts = swap(copies(part, row_size), "row")
            parts = parts.reshape((-1, 2, Z_SIZE) + part.shape)
            solved.append(parts.transpose(0, 2, 3, 1, 4).reshape(-1, column_count))

    trail_acc = None
    for block_row in range(step_count):
        contrib = jnp.einsum(
            "nc,mrn->cmr",
            solved[block_row],
            trail_panel[:, :, block_row, :],
            precision=HIGHEST_PREC,
        )
        trail_acc = contrib if trail_acc is None else trail_acc + contrib
    shared = reduce_scatter(trail_acc.reshape(column_count, -1), "col", col_size)
    own_width = shared.shape[0]
    shared = shared.reshape(own_width, trail_count, local_rows).transpose(1, 2, 0)
    own_sides = lax.dynamic_slice_in_dim(
        right_sides[step_count:], lax.axis_index("col") * own_width, own_width, 2
    )
    trail_rest = own_sides - shared
    out_width = column_count // row_size
    outs = [lax.dynamic_slice_in_dim(s, row * out_width, out_width, 1) for s in solved]
    return (jnp.stack(outs), trail_rest)


def solution(mesh):
    placed = (
        P(None, "row", None),
        P(None, "col", "row"),
        P(None, "row", "col"),
        P(None, "row", None, "col"),
    )
    return jax.shard_map(
        shards,
        mesh=mesh,
        in_specs=placed,
        out_specs=(P(None, "col", "row"), P(None, "row", "col")),
        check_vma=False,
    )
```

```python
import jax
import jax.numpy as jnp
from jax import lax
from jax.sharding import PartitionSpec as P

HIGHEST_PREC = lax.Precision.HIGHEST
CORES = 2


def pair_index(block_row, prior_row):
    return block_row * (block_row - 1) // 2 + prior_row


def contract(left, right, axes):
    return lax.dot_general(
        left,
        right,
        (((axes[0],), (axes[1],)), ((), ())),
        precision=HIGHEST_PREC,
        preferred_element_type=jnp.float32,
    )


def swap(parts, axis, groups=None):
    return lax.all_to_all(parts, axis, 0, 0, axis_index_groups=groups, tiled=True)


def copies(part, count):
    return jnp.broadcast_to(part[None], (count,) + part.shape)


def halves_swapped(value):
    return jnp.roll(value, value.shape[-1] // 2, value.ndim - 1)


def shards(right_sides, diag_inverse, lower_blocks, trail_panel):
    step_count = diag_inverse.shape[0]
    pair_count = lower_blocks.shape[0]
    trail_count = trail_panel.shape[0]
    local_rows = right_sides.shape[1]
    column_count = right_sides.shape[2]
    block_width = lower_blocks.shape[2]
    row_size = lax.axis_size("row")
    col_size = lax.axis_size("col")
    members = row_size // 2
    chips = col_size // CORES
    half = column_count // 2
    quarter = half // 2
    row = lax.axis_index("row")
    col = lax.axis_index("col")
    parity = row % 2
    core = col % CORES
    row_groups = [[r for r in range(row_size) if r % 2 == g] for g in range(2)]
    chip_groups = [[c for c in range(col_size) if c % CORES == g] for g in range(CORES)]
    row_pairs = [(r, r ^ 1) for r in range(row_size)]
    core_pairs = [(c, c ^ 1) for c in range(col_size)]
    low = lax.broadcasted_iota(jnp.int32, (1, half), 1) < quarter

    def from_row(value):
        return lax.ppermute(value, "row", row_pairs)

    def from_core(value):
        return lax.ppermute(value, "col", core_pairs)

    def gathered(own):
        by_row = from_row(own)
        return own, by_row, from_core(own), from_core(by_row)

    own_diag = diag_inverse.transpose(0, 2, 1)

    own_sides = lax.dynamic_slice_in_dim(right_sides[1:step_count], core * half, half, 2)
    sides = jnp.concatenate([own_sides, from_row(own_sides)], 1)
    sides = jnp.where(low == (parity == 0), sides, halves_swapped(sides))
    batches = []
    for block_row in range(1, step_count):
        start = pair_index(block_row, 0)
        own = [lower_blocks[start : start + block_row], own_diag[block_row : block_row + 1]]
        batches.append(gathered(jnp.concatenate(own)))

    def lower_of(block_row, prior_row):
        return jnp.concatenate([b[prior_row] for b in batches[block_row - 1]])

    def diag_of(block_row):
        return jnp.concatenate([b[block_row] for b in batches[block_row - 1]])

    def update_of(block_row, prior_row):
        both = contract(lower_of(block_row, prior_row), solved[prior_row], (1, 0))
        rows = 2 * local_rows
        return jnp.where(low, both[:rows], both[rows:])

    def by_core(value):
        other = from_core(value)
        straight = jnp.where(low, value, other)
        turned = halves_swapped(jnp.where(low, value, other))
        return jnp.where(core == 0, straight, turned)

    local_term = contract(own_diag[0], right_sides[0], (0, 0))
    parts = local_term.reshape(row_size, block_width // row_size, column_count)
    part = swap(parts, "row").sum(0)
    mine = lax.dynamic_slice_in_dim(part, core * half, half, 1)
    other = from_core(lax.dynamic_slice_in_dim(part, (1 - core) * half, half, 1))
    for_even = jnp.where(low, mine, halves_swapped(other))
    for_odd = jnp.where(low, halves_swapped(mine), other)
    parts = copies(jnp.stack([for_even, for_odd]), members).reshape(row_size, -1, half)
    solved = [swap(parts, "row").reshape(block_width, half)]

    for block_row in range(1, step_count):
        update = None
        for prior_row in range(block_row):
            term = update_of(block_row, prior_row)
            update = term if update is None else update + term
        total = swap(copies(update, chips), "col", chip_groups).sum(0)
        current = sides[block_row - 1] - (total + halves_swapped(total))
        zero = jnp.zeros_like(current)
        spread = jnp.concatenate([jnp.where(low, current, zero), jnp.where(low, zero, current)])
        local_term = contract(diag_of(block_row), spread, (0, 0))
        parts = local_term.reshape(members, block_width // members, half)
        part = swap(parts, "row", row_groups).sum(0)
        if block_row < step_count - 1:
            parts = swap(copies(part, members), "row", row_groups)
            solved.append(parts.reshape(block_width, half))

    wholes = []
    for value in solved:
        straight = by_core(value)
        other = from_row(straight)
        wholes.append(
            (
                jnp.where(parity == 0, straight, other),
                jnp.where(parity == 0, other, straight),
            )
        )
    parts = swap(copies(by_core(part), row_size), "row")
    parts = parts.reshape(members, 2, -1, half)
    wholes.append(tuple(parts[:, g].reshape(block_width, half) for g in range(2)))

    shared_parts = []
    for g in range(2):
        acc = None
        for block_row in range(step_count):
            contrib = jnp.einsum(
                "nc,mrn->cmr",
                wholes[block_row][g],
                trail_panel[:, :, block_row, :],
                precision=HIGHEST_PREC,
            )
            acc = contrib if acc is None else acc + contrib
        shared_parts.append(acc.reshape(CORES, chips // 2, -1, trail_count * local_rows))
    shared = jnp.stack(shared_parts, 1).reshape(col_size, -1, trail_count * local_rows)
    shared = swap(shared, "col").sum(0)
    own_width = shared.shape[0]
    shared = shared.reshape(own_width, trail_count, local_rows).transpose(1, 2, 0)
    below = lax.dynamic_slice_in_dim(right_sides[step_count:], col * own_width, own_width, 2)
    trail_rest = below - shared

    out_width = column_count // row_size
    first = row * out_width
    place = first % quarter + first // half * quarter
    odd = first // quarter % 2 == 1
    outs = []
    for even_part, odd_part in wholes:
        picked = [lax.dynamic_slice_in_dim(v, place, out_width, 1) for v in (even_part, odd_part)]
        outs.append(jnp.where(odd, picked[1], picked[0]))
    return (jnp.stack(outs), trail_rest)


def solution(mesh):
    placed = (
        P(None, "row", None),
        P(None, "col", "row"),
        P(None, "row", "col"),
        P(None, "row", None, "col"),
    )
    return jax.shard_map(
        shards,
        mesh=mesh,
        in_specs=placed,
        out_specs=(P(None, "col", "row"), P(None, "row", "col")),
        check_vma=False,
    )
```

```python
import jax
import jax.numpy as jnp
from jax import lax
from jax.sharding import PartitionSpec as P

PRECISION = lax.Precision.HIGHEST
CORES = 2


def pair_index(block_row, prior_row):
    return block_row * (block_row - 1) // 2 + prior_row


def contract(left, right, axes):
    return lax.dot_general(
        left,
        right,
        (((axes[0],), (axes[1],)), ((), ())),
        precision=PRECISION,
        preferred_element_type=jnp.float32,
    )


def swap(parts, axis, groups=None):
    return lax.all_to_all(parts, axis, 0, 0, axis_index_groups=groups, tiled=True)


def copies(part, count):
    return jnp.broadcast_to(part[None], (count,) + part.shape)


def halves_swapped(value):
    return jnp.roll(value, value.shape[-1] // 2, value.ndim - 1)


def tie(*values):
    return lax.optimization_barrier(values)


def shards(right_sides, diag_inverse, lower_blocks, trail_panel):
    step_count = diag_inverse.shape[0]
    trail_count = trail_panel.shape[0]
    local_rows = right_sides.shape[1]
    column_count = right_sides.shape[2]
    width = lower_blocks.shape[2]
    row_size = lax.axis_size("row")
    col_size = lax.axis_size("col")
    members = row_size // 2
    chips = col_size // CORES
    half = column_count // 2
    quarter = half // 2
    row = lax.axis_index("row")
    col = lax.axis_index("col")
    parity = row % 2
    core = col % CORES
    row_groups = [[r for r in range(row_size) if r % 2 == g] for g in range(2)]
    chip_groups = [[c for c in range(col_size) if c % CORES == g] for g in range(CORES)]
    row_pairs = [(r, r ^ 1) for r in range(row_size)]
    core_pairs = [(c, c ^ 1) for c in range(col_size)]
    low = lax.broadcasted_iota(jnp.int32, (1, half), 1) < quarter

    def from_row(value):
        return lax.ppermute(value, "row", row_pairs)

    def from_core(value):
        return lax.ppermute(value, "col", core_pairs)

    own_diag = diag_inverse.transpose(0, 2, 1)
    own_sides = lax.dynamic_slice_in_dim(right_sides[:step_count], parity * half, half, 2)
    sent_sides = lax.dynamic_slice_in_dim(right_sides[:step_count], (1 - parity) * half, half, 2)

    def side_of(block_row, received):
        value = jnp.concatenate([own_sides[block_row], received])
        return jnp.where(low == (core == 0), value, halves_swapped(value))

    def matrix(pieces, index):
        return jnp.concatenate([p[:, index * width : (index + 1) * width] for p in pieces])

    def update_of(matrices, solved_block):
        both = contract(matrices, solved_block, (1, 0))
        rows = 2 * local_rows
        return jnp.where(low, both[:rows], both[rows:])

    def partial_of(matrices, current):
        zero = jnp.zeros_like(current)
        spread = jnp.concatenate([jnp.where(low, current, zero), jnp.where(low, zero, current)])
        return contract(matrices, spread, (0, 0))

    def scattered(value):
        parts = value.reshape(members, width // members, half)
        return swap(parts, "row", row_groups)

    def gathered(part):
        return swap(copies(part, members), "row", row_groups)

    def summed(update):
        return swap(copies(update, chips), "col", chip_groups)

    def current_of(side, parts):
        total = parts.sum(0)
        return side - (total + halves_swapped(total))

    def by_core(value, other):
        straight = jnp.where(low, value, other)
        return jnp.where(core == 0, straight, halves_swapped(straight))

    def by_parity(value, other):
        return jnp.concatenate(
            [jnp.where(parity == 0, value, other), jnp.where(parity == 0, other, value)], 1
        )

    trail = [trail_panel[:, :, j, :] for j in range(step_count)]

    def below_of(whole, block_row):
        return jnp.einsum("nc,mrn->cmr", whole, trail[block_row], precision=PRECISION)

    front = jnp.concatenate([own_diag[0], sent_sides[0]], 1)
    front_row = from_row(front)
    front_core = from_core(own_diag[0])
    front_both = from_core(front_row)
    pieces = [own_diag[0], front_row, front_core, front_both]
    current = side_of(0, front_row[:, width:])
    local_term = partial_of(matrix(pieces, 0), current)
    parts = scattered(local_term)

    first = jnp.concatenate(
        [lower_blocks[0], own_diag[1]] + [sent_sides[i] for i in range(1, step_count)], 1
    )
    first, _ = tie(first, front_both)
    first_row, first_core = from_row(first), from_core(first[:, : 2 * width])
    parts, first_row, first_core = tie(parts, first_row, first_core)
    part = parts.sum(0)

    second = jnp.concatenate([lower_blocks[1], lower_blocks[2], own_diag[2]], 1)
    second, _ = tie(second, first_row)
    first_both = from_core(first_row)
    second_row, second_core = from_row(second), from_core(second)
    parts = gathered(part)
    parts, first_both, second_row, second_core = tie(parts, first_both, second_row, second_core)
    solved_0 = parts.reshape(width, half)
    firsts = [first, first_row, first_core, first_both]

    sides = [
        side_of(i, first_row[:, 2 * width + (i - 1) * half : 2 * width + i * half])
        for i in range(1, step_count)
    ]
    parts = summed(update_of(matrix(firsts, 0), solved_0))
    third = jnp.concatenate([lower_blocks[3], lower_blocks[4], lower_blocks[5], own_diag[3]], 1)
    third, _ = tie(third, solved_0)
    third_row, third_core = from_row(third), from_core(third)
    second_both = from_core(second_row)
    current = current_of(sides[0], parts)
    parts = scattered(partial_of(matrix(firsts, 1), current))
    core_0 = from_core(solved_0)
    parts, second_both, third_row, third_core, core_0 = tie(
        parts, second_both, third_row, third_core, core_0
    )
    part = parts.sum(0)
    seconds = [second, second_row, second_core, second_both]
    pending_2 = update_of(matrix(seconds, 0), solved_0)
    straight_0 = by_core(solved_0, core_0)
    whole_0 = by_parity(straight_0, from_row(straight_0))
    third_both = from_core(third_row)
    parts = gathered(part)
    parts, whole_0, third_both, pending_2 = tie(parts, whole_0, third_both, pending_2)
    solved_1 = parts.reshape(width, half)
    thirds = [third, third_row, third_core, third_both]

    parts = summed(pending_2 + update_of(matrix(seconds, 1), solved_1))
    current = current_of(sides[1], parts)
    parts = scattered(partial_of(matrix(seconds, 2), current))
    below = below_of(whole_0, 0)
    core_1 = from_core(solved_1)
    parts, below, core_1 = tie(parts, below, core_1)
    part = parts.sum(0)
    straight_1 = by_core(solved_1, core_1)
    whole_1 = by_parity(straight_1, from_row(straight_1))
    pending_3 = update_of(matrix(thirds, 0), solved_0) + update_of(matrix(thirds, 1), solved_1)
    parts = gathered(part)
    parts, whole_1, pending_3 = tie(parts, whole_1, pending_3)
    solved_2 = parts.reshape(width, half)

    parts = summed(pending_3 + update_of(matrix(thirds, 2), solved_2))
    core_2 = from_core(solved_2)
    current = current_of(sides[2], parts)
    parts = scattered(partial_of(matrix(thirds, 3), current))
    straight_2 = by_core(solved_2, core_2)
    row_2 = from_row(straight_2)
    below = below + below_of(whole_1, 1)
    parts, below, row_2 = tie(parts, below, row_2)
    part = parts.sum(0)
    part = by_core(part, from_core(part))
    parts = swap(copies(part, row_size), "row")
    whole_2 = by_parity(straight_2, row_2)
    below = below + below_of(whole_2, 2)
    parts, below = tie(parts, below)
    parts = parts.reshape(members, 2, width // members, half)
    whole_3 = parts.transpose(0, 2, 1, 3).reshape(width, column_count)

    below = below + below_of(whole_3, 3)
    shared = swap(below.reshape(column_count, -1), "col")
    own_width = column_count // col_size
    shared = shared.reshape(col_size, own_width, -1).sum(0)
    shared = shared.reshape(own_width, trail_count, local_rows).transpose(1, 2, 0)
    own_below = lax.dynamic_slice_in_dim(right_sides[step_count:], col * own_width, own_width, 2)
    trail_rest = own_below - shared

    out_width = column_count // row_size
    outs = [
        lax.dynamic_slice_in_dim(whole, row * out_width, out_width, 1)
        for whole in (whole_0, whole_1, whole_2, whole_3)
    ]
    return (jnp.stack(outs), trail_rest)


def solution(mesh):
    placed = (
        P(None, "row", None),
        P(None, "col", "row"),
        P(None, "row", "col"),
        P(None, "row", None, "col"),
    )
    return jax.shard_map(
        shards,
        mesh=mesh,
        in_specs=placed,
        out_specs=(P(None, "col", "row"), P(None, "row", "col")),
        check_vma=False,
    )
```

```python
import jax
import jax.numpy as jnp
from jax import lax
from jax.sharding import PartitionSpec as P

PRECISION = lax.Precision.HIGHEST
CORES = 2


def pair_index(block_row, prior_row):
    return block_row * (block_row - 1) // 2 + prior_row


def contract(left, right, axes):
    return lax.dot_general(
        left,
        right,
        (((axes[0],), (axes[1],)), ((), ())),
        precision=PRECISION,
        preferred_element_type=jnp.float32,
    )


def swap(parts, axis, groups=None):
    return lax.all_to_all(parts, axis, 0, 0, axis_index_groups=groups, tiled=True)


def copies(part, count):
    return jnp.broadcast_to(part[None], (count,) + part.shape)


def halves_swapped(value):
    return jnp.roll(value, value.shape[-1] // 2, value.ndim - 1)


def window(parts, axis, groups=None, inputs=(), work=None):
    if work is None:
        return swap(parts, axis, groups), ()
    parts, inputs = lax.optimization_barrier((parts, inputs))
    return lax.optimization_barrier((swap(parts, axis, groups), work(*inputs)))


def shards(right_sides, diag_inverse, lower_blocks, trail_panel):
    step_count = diag_inverse.shape[0]
    trail_count = trail_panel.shape[0]
    local_rows = right_sides.shape[1]
    column_count = right_sides.shape[2]
    width = lower_blocks.shape[2]
    row_size = lax.axis_size("row")
    col_size = lax.axis_size("col")
    members = row_size // 2
    chips = col_size // CORES
    half = column_count // 2
    quarter = half // 2
    row = lax.axis_index("row")
    col = lax.axis_index("col")
    parity = row % 2
    core = col % CORES
    row_groups = [[r for r in range(row_size) if r % 2 == g] for g in range(2)]
    chip_groups = [[c for c in range(col_size) if c % CORES == g] for g in range(CORES)]
    row_pairs = [(r, r ^ 1) for r in range(row_size)]
    core_pairs = [(c, c ^ 1) for c in range(col_size)]
    low = lax.broadcasted_iota(jnp.int32, (1, half), 1) < quarter

    def from_row(value):
        return lax.ppermute(value, "row", row_pairs)

    def from_core(value):
        return lax.ppermute(value, "col", core_pairs)

    own_diag = diag_inverse.transpose(0, 2, 1)
    own_sides = lax.dynamic_slice_in_dim(right_sides[:step_count], parity * half, half, 2)
    sent_sides = lax.dynamic_slice_in_dim(right_sides[:step_count], (1 - parity) * half, half, 2)

    def side_of(block_row, received):
        value = jnp.concatenate([own_sides[block_row], received])
        return jnp.where(low == (core == 0), value, halves_swapped(value))

    def matrix(pieces, index):
        return jnp.concatenate([p[:, index * width : (index + 1) * width] for p in pieces])

    def update_of(matrices, solved_block):
        both = contract(matrices, solved_block, (1, 0))
        rows = 2 * local_rows
        return jnp.where(low, both[:rows], both[rows:])

    def partial_of(matrices, current):
        zero = jnp.zeros_like(current)
        spread = jnp.concatenate([jnp.where(low, current, zero), jnp.where(low, zero, current)])
        return contract(matrices, spread, (0, 0))

    def scattered(value, inputs=(), work=None):
        parts = value.reshape(members, width // members, half)
        got, done = window(parts, "row", row_groups, inputs, work)
        return got.sum(0), done

    def gathered(part, inputs=(), work=None):
        got, done = window(copies(part, members), "row", row_groups, inputs, work)
        return got.reshape(width, half), done

    def summed(update, inputs=(), work=None):
        return window(copies(update, chips), "col", chip_groups, inputs, work)

    def current_of(side, parts):
        total = parts.sum(0)
        return side - (total + halves_swapped(total))

    def by_core(value, other):
        straight = jnp.where(low, value, other)
        return jnp.where(core == 0, straight, halves_swapped(straight))

    def by_parity(value, other):
        return jnp.concatenate(
            [jnp.where(parity == 0, value, other), jnp.where(parity == 0, other, value)], 1
        )

    def below_of(whole, trail_block):
        return jnp.einsum("nc,mrn->cmr", whole, trail_block, precision=PRECISION)

    front = jnp.concatenate([own_diag[0], sent_sides[0]], 1)
    front_row = from_row(front)
    front_core = from_core(own_diag[0])
    first = jnp.concatenate(
        [lower_blocks[0], own_diag[1]] + [sent_sides[i] for i in range(1, step_count)], 1
    )
    first, _ = lax.optimization_barrier((first, front))
    first_row = from_row(first)
    front_both = from_core(front_row)

    current = side_of(0, front_row[:, width:])
    diag_0 = matrix([own_diag[0], front_row, front_core, front_both], 0)
    part, firsts = scattered(
        partial_of(diag_0, current),
        (first, first_row),
        lambda own, by_row: (own, by_row, from_core(own[:, : 2 * width]), from_core(by_row)),
    )
    solved_0, (lower_10, diag_1, sides, trail) = gathered(
        part,
        (firsts, trail_panel),
        lambda pieces, panel: (
            matrix(pieces, 0),
            matrix(pieces, 1),
            [
                side_of(i, pieces[1][:, 2 * width + (i - 1) * half : 2 * width + i * half])
                for i in range(1, step_count)
            ],
            [panel[:, :, j, :] for j in range(step_count)],
        ),
    )

    second = jnp.concatenate([lower_blocks[1], lower_blocks[2], lower_blocks[3], own_diag[2]], 1)
    parts, (second_row, core_0) = summed(
        update_of(lower_10, solved_0),
        (second, solved_0),
        lambda own, block: (from_row(own), from_core(block)),
    )
    current = current_of(sides[0], parts)
    part, seconds = scattered(
        partial_of(diag_1, current),
        (second, second_row),
        lambda own, by_row: (own, by_row, from_core(own), from_core(by_row)),
    )
    solved_1, (lower_21, diag_2, pending_2, lower_30, straight_0) = gathered(
        part,
        (seconds, solved_0, core_0),
        lambda pieces, block, other: (
            matrix(pieces, 1),
            matrix(pieces, 3),
            update_of(matrix(pieces, 0), block),
            matrix(pieces, 2),
            by_core(block, other),
        ),
    )

    third = jnp.concatenate([lower_blocks[4], lower_blocks[5], own_diag[3]], 1)
    parts, (third_row, core_1, row_0) = summed(
        pending_2 + update_of(lower_21, solved_1),
        (third, solved_1, straight_0),
        lambda own, block, other: (from_row(own), from_core(block), from_row(other)),
    )
    current = current_of(sides[1], parts)
    part, (thirds, pending_3, straight_1) = scattered(
        partial_of(diag_2, current),
        (third, third_row, lower_30, solved_0, solved_1, core_1),
        lambda own, by_row, lower, block, last, other: (
            (own, by_row, from_core(own), from_core(by_row)),
            update_of(lower, block),
            by_core(last, other),
        ),
    )
    solved_2, (lower_32, diag_3, pending_3, whole_0, below) = gathered(
        part,
        (thirds, pending_3, solved_1, straight_0, row_0, trail[0]),
        lambda pieces, pending, block, straight, other, trail_block: (
            matrix(pieces, 1),
            matrix(pieces, 2),
            pending + update_of(matrix(pieces, 0), block),
            by_parity(straight, other),
            below_of(by_parity(straight, other), trail_block),
        ),
    )

    parts, (row_1, core_2) = summed(
        pending_3 + update_of(lower_32, solved_2),
        (straight_1, solved_2),
        lambda straight, block: (from_row(straight), from_core(block)),
    )
    current = current_of(sides[2], parts)
    part, (row_2, straight_2, whole_1, below) = scattered(
        partial_of(diag_3, current),
        (solved_2, core_2, straight_1, row_1, trail[1], below),
        lambda block, other, straight, by_row, trail_block, total: (
            from_row(by_core(block, other)),
            by_core(block, other),
            by_parity(straight, by_row),
            total + below_of(by_parity(straight, by_row), trail_block),
        ),
    )
    part = by_core(part, from_core(part))
    parts, (whole_2, below) = window(
        copies(part, row_size),
        "row",
        None,
        (straight_2, row_2, trail[2], below),
        lambda straight, other, trail_block, total: (
            by_parity(straight, other),
            total + below_of(by_parity(straight, other), trail_block),
        ),
    )
    parts = parts.reshape(members, 2, width // members, half)
    whole_3 = parts.transpose(0, 2, 1, 3).reshape(width, column_count)

    below = below + below_of(whole_3, trail[3])
    shared = swap(below.reshape(column_count, -1), "col")
    own_width = column_count // col_size
    shared = shared.reshape(col_size, own_width, -1).sum(0)
    shared = shared.reshape(own_width, trail_count, local_rows).transpose(1, 2, 0)
    own_below = lax.dynamic_slice_in_dim(right_sides[step_count:], col * own_width, own_width, 2)
    trail_rest = own_below - shared

    out_width = column_count // row_size
    outs = [
        lax.dynamic_slice_in_dim(whole, row * out_width, out_width, 1)
        for whole in (whole_0, whole_1, whole_2, whole_3)
    ]
    return (jnp.stack(outs), trail_rest)


def solution(mesh):
    placed = (
        P(None, "row", None),
        P(None, "col", "row"),
        P(None, "row", "col"),
        P(None, "row", None, "col"),
    )
    return jax.shard_map(
        shards,
        mesh=mesh,
        in_specs=placed,
        out_specs=(P(None, "col", "row"), P(None, "row", "col")),
        check_vma=False,
    )
```

```python
import jax
import jax.numpy as jnp
from jax import lax
from jax.sharding import PartitionSpec as P

PRECISION = lax.Precision.HIGHEST


def contract(left, right, axes):
    return lax.dot_general(
        left,
        right,
        (((axes[0],), (axes[1],)), ((), ())),
        precision=PRECISION,
        preferred_element_type=jnp.float32,
    )


def swap(parts, axis, groups=None):
    return lax.all_to_all(parts, axis, 0, 0, axis_index_groups=groups, tiled=True)


def copies(part, count):
    return jnp.broadcast_to(part[None], (count,) + part.shape)


def by_deadline(*values):
    return lax.optimization_barrier(values)


def shards(right_sides, diag_inverse, lower_blocks, trail_panel):
    step_count = diag_inverse.shape[0]
    trail_count = trail_panel.shape[0]
    local_rows = right_sides.shape[1]
    column_count = right_sides.shape[2]
    width = lower_blocks.shape[2]
    row_size = lax.axis_size("row")
    col_size = lax.axis_size("col")
    members = row_size // 2
    half = column_count // 2
    row = lax.axis_index("row")
    col = lax.axis_index("col")
    parity = row % 2
    row_groups = [[r for r in range(row_size) if r % 2 == g] for g in range(2)]
    row_pairs = [(r, r ^ 1) for r in range(row_size)]

    def from_partner(value):
        return lax.ppermute(value, "row", row_pairs)

    def half_of(value, which):
        return lax.dynamic_slice_in_dim(value, which * half, half, value.ndim - 1)

    def both(own, received, index):
        return jnp.concatenate([v[:, index * width : (index + 1) * width] for v in (own, received)])

    def by_parity(value, other):
        return jnp.concatenate(
            [jnp.where(parity == 0, value, other), jnp.where(parity == 0, other, value)], 1
        )

    def scattered(value):
        parts = value.reshape(members, width // members, half)
        return swap(parts, "row", row_groups)

    def gathered(part):
        return swap(copies(part, members), "row", row_groups)

    def summed(update):
        return swap(copies(update, col_size), "col")

    def below_of(whole, trail_block):
        return jnp.einsum("nc,mrn->cmr", whole, trail_block, precision=PRECISION)

    own_diag = diag_inverse.transpose(0, 2, 1)
    later = right_sides[1:step_count]
    own_sides = half_of(later, parity)
    sent_sides = half_of(later, 1 - parity)
    trail = [trail_panel[:, :, j, :] for j in range(step_count)]

    first = jnp.concatenate(
        [lower_blocks[0], own_diag[1]] + [sent_sides[i] for i in range(step_count - 1)], 1
    )
    first_got = from_partner(first)
    second = jnp.concatenate(
        [lower_blocks[1], lower_blocks[2], lower_blocks[3], lower_blocks[4], own_diag[2]], 1
    )
    second_got = from_partner(second)
    third = jnp.concatenate([lower_blocks[5], own_diag[3]], 1)
    third_got = from_partner(third)

    local_term = contract(own_diag[0], right_sides[0], (0, 0))
    parts = swap(local_term.reshape(row_size, width // row_size, column_count), "row")
    parts, first_got = by_deadline(parts, first_got)
    lower_10, diag_1 = both(first, first_got, 0), both(first, first_got, 1)
    sides = [
        jnp.concatenate(
            [own_sides[i], first_got[:, 2 * width + i * half : 2 * width + (i + 1) * half]]
        )
        for i in range(step_count - 1)
    ]
    parts = swap(copies(parts.sum(0), row_size), "row")
    parts, lower_10, diag_1, sides = by_deadline(parts, lower_10, diag_1, sides)
    whole_0 = parts.reshape(width, column_count)
    solved_0 = half_of(whole_0, parity)

    parts = summed(contract(lower_10, solved_0, (1, 0)))
    parts, second_got = by_deadline(parts, second_got)
    current = sides[0] - parts.sum(0)
    below = below_of(whole_0, trail[0])
    parts = scattered(contract(diag_1, current, (0, 0)))
    lower_20, lower_21 = both(second, second_got, 0), both(second, second_got, 1)
    lower_30, lower_31 = both(second, second_got, 2), both(second, second_got, 3)
    diag_2 = both(second, second_got, 4)
    parts, lower_21, lower_31, diag_2 = by_deadline(parts, lower_21, lower_31, diag_2)
    pending_2 = contract(lower_20, solved_0, (1, 0))
    pending_3 = contract(lower_30, solved_0, (1, 0))
    parts = gathered(parts.sum(0))
    parts, pending_2, pending_3, below, trail = by_deadline(
        parts, pending_2, pending_3, below, trail
    )
    solved_1 = parts.reshape(width, half)

    parts = summed(pending_2 + contract(lower_21, solved_1, (1, 0)))
    other_1 = from_partner(solved_1)
    parts, third_got, other_1 = by_deadline(parts, third_got, other_1)
    current = sides[1] - parts.sum(0)
    parts = scattered(contract(diag_2, current, (0, 0)))
    lower_32, diag_3 = both(third, third_got, 0), both(third, third_got, 1)
    pending_3 = pending_3 + contract(lower_31, solved_1, (1, 0))
    parts, lower_32, diag_3, pending_3 = by_deadline(parts, lower_32, diag_3, pending_3)
    parts = gathered(parts.sum(0))
    whole_1 = by_parity(solved_1, other_1)
    below = below + below_of(whole_1, trail[1])
    parts, below = by_deadline(parts, below)
    solved_2 = parts.reshape(width, half)

    parts = summed(pending_3 + contract(lower_32, solved_2, (1, 0)))
    other_2 = from_partner(solved_2)
    current = sides[2] - parts.sum(0)
    parts = scattered(contract(diag_3, current, (0, 0)))
    parts, other_2 = by_deadline(parts, other_2)
    parts = swap(copies(parts.sum(0), row_size), "row")
    whole_2 = by_parity(solved_2, other_2)
    below = below + below_of(whole_2, trail[2])
    parts, below = by_deadline(parts, below)
    parts = parts.reshape(members, 2, width // members, half)
    whole_3 = parts.transpose(0, 2, 1, 3).reshape(width, column_count)

    below = below + below_of(whole_3, trail[3])
    shared = swap(below.reshape(column_count, -1), "col")
    own_width = column_count // col_size
    shared = shared.reshape(col_size, own_width, -1).sum(0)
    shared = shared.reshape(own_width, trail_count, local_rows).transpose(1, 2, 0)
    own_below = lax.dynamic_slice_in_dim(right_sides[step_count:], col * own_width, own_width, 2)
    trail_rest = own_below - shared

    out_width = column_count // row_size
    outs = [
        lax.dynamic_slice_in_dim(whole, row * out_width, out_width, 1)
        for whole in (whole_0, whole_1, whole_2, whole_3)
    ]
    return (jnp.stack(outs), trail_rest)


def solution(mesh):
    placed = (
        P(None, "row", None),
        P(None, "col", "row"),
        P(None, "row", "col"),
        P(None, "row", None, "col"),
    )
    return jax.shard_map(
        shards,
        mesh=mesh,
        in_specs=placed,
        out_specs=(P(None, "col", "row"), P(None, "row", "col")),
        check_vma=False,
    )
```

```python
import jax
import jax.numpy as jnp
from jax import lax
from jax.sharding import PartitionSpec as P

PRECISION = lax.Precision.HIGHEST
X_NEAR, X_FAR, CORE = 2, 6, 1
PACK = 4
Z_SIZE = 8


def pair_index(block_row, prior_row):
    return block_row * (block_row - 1) // 2 + prior_row


def contract(left, right, axes):
    return lax.dot_general(
        left,
        right,
        (((axes[0],), (axes[1],)), ((), ())),
        precision=PRECISION,
        preferred_element_type=jnp.float32,
    )


def swap(parts, axis):
    return lax.all_to_all(parts, axis, 0, 0, tiled=True)


def copies(part, count):
    return jnp.broadcast_to(part[None], (count,) + part.shape)


def by_deadline(*values):
    return lax.optimization_barrier(values)


def shards(right_sides, diag_inverse, lower_blocks, trail_panel):
    step_count = diag_inverse.shape[0]
    trail_count = trail_panel.shape[0]
    local_rows = right_sides.shape[1]
    column_count = right_sides.shape[2]
    width = lower_blocks.shape[2]
    row_size = lax.axis_size("row")
    col_size = lax.axis_size("col")
    own_width = column_count // col_size
    lanes = PACK * own_width
    piece_rows = width // row_size
    row = lax.axis_index("row")
    col = lax.axis_index("col")
    lane_block = lax.broadcasted_iota(jnp.int32, (1, lanes), 1) // own_width

    def from_col(value, difference):
        return lax.ppermute(value, "col", [(c, c ^ difference) for c in range(col_size)])

    def near(own):
        return jnp.concatenate([own, from_col(own, X_NEAR)], 1)

    def far(pair):
        return jnp.concatenate([pair, from_col(pair, X_FAR)], 1)

    def other_core(four):
        return (four, from_col(four, CORE))

    def folded(value):
        value = value + jnp.roll(value, 2 * own_width, value.ndim - 1)
        return value + jnp.roll(value, own_width, value.ndim - 1)

    def own_sides(sides):
        start = col // PACK * lanes
        picked = lax.dynamic_slice_in_dim(sides, start, lanes, sides.ndim - 1)
        return folded(jnp.where(lane_block == col % PACK, picked, 0.0))

    def product(matrices, solved):
        total = None
        for matrix, block in zip(matrices, solved):
            n, pack, rows, depth = matrix.shape
            term = contract(matrix.reshape(n * pack * rows, depth), block, (1, 0))
            total = term if total is None else total + term
        total = total.reshape(n, pack, rows, lanes)
        picked = [jnp.where(lane_block == b, total[:, b], 0.0) for b in range(pack)]
        return sum(picked[1:], picked[0])

    def scattered(matrices, current):
        spread = jnp.concatenate([jnp.where(lane_block == b, current, 0.0) for b in range(PACK)])
        terms = [
            contract(m.reshape(-1, width), spread, (0, 0)).reshape(row_size, 1, piece_rows, lanes)
            for m in matrices
        ]
        return swap(jnp.concatenate(terms, 1), "row")

    def solved_of(parts):
        return [parts[:, g].reshape(width, lanes) for g in range(2)]

    def out_of(solved):
        difference = (row // Z_SIZE) ^ col
        far_bit = difference // 4 % 2
        near_bit = (difference // 2 % 2) ^ far_bit
        place = (far_bit * 2 + near_bit) * own_width + row % Z_SIZE * (own_width // Z_SIZE)
        picked = [
            lax.dynamic_slice_in_dim(s, place, own_width // Z_SIZE, 1).T for s in solved
        ]
        return jnp.where(difference % 2 == 0, picked[0], picked[1])

    def sent_out(values):
        pairs = []
        for r in range(row_size):
            for c in range(col_size):
                target = (c * Z_SIZE + r % Z_SIZE) * col_size + r // Z_SIZE
                pairs.append((r * col_size + c, target))
        return lax.ppermute(values, ("row", "col"), pairs)

    own_diag = diag_inverse.transpose(0, 2, 1)
    batches = []
    for block_row in range(1, step_count):
        start = pair_index(block_row, 0)
        own = [lower_blocks[start : start + block_row], own_diag[block_row : block_row + 1]]
        batches.append(jnp.concatenate(own)[:, None])
    trail_own = trail_panel.transpose(2, 0, 1, 3).reshape(step_count, trail_count, 1, local_rows, width)
    trails = [
        trail_own[j : j + 2].reshape(2 * trail_count, 1, local_rows, width)
        for j in range(0, step_count, 2)
    ]
    first, second, third = batches

    local_term = contract(own_diag[0], right_sides[0], (0, 0))
    parts = swap(local_term.reshape(row_size, piece_rows, column_count), "row")
    first = far(near(first))
    parts, first = by_deadline(parts, first)
    part = parts.sum(0).reshape(piece_rows, col_size, own_width).transpose(1, 0, 2)
    part = swap(part, "col").reshape(2, 2, 2, piece_rows, own_width)
    for axis, bit in ((0, 4), (1, 2), (2, 1)):
        part = jnp.where(col // bit % 2 == 1, jnp.flip(part, axis), part)
    part = jnp.stack(
        [
            jnp.concatenate([part[0, 0, g], part[0, 1, g], part[1, 1, g], part[1, 0, g]], 1)
            for g in range(2)
        ]
    )
    parts = swap(copies(part, row_size), "row")
    first = other_core(first)
    second = near(second)
    sides = [own_sides(right_sides[i]) for i in range(1, step_count)]
    parts, first, second, sides = by_deadline(parts, first, second, sides)
    solved_0 = solved_of(parts)

    current = sides[0] - folded(product([m[:1] for m in first], solved_0)[0])
    parts = scattered([m[1] for m in first], current)
    second = far(second)
    second = other_core(second)
    third = near(third)
    parts, second, third = by_deadline(parts, second, third)
    part = parts.sum(0)
    parts = swap(copies(part, row_size), "row")
    third = far(third)
    trails[0] = near(trails[0])
    pending = product([m[:1] for m in second], solved_0)
    parts, third, trails[0], pending = by_deadline(parts, third, trails[0], pending)
    solved_1 = solved_of(parts)

    current = sides[1] - folded((pending + product([m[1:2] for m in second], solved_1))[0])
    parts = scattered([m[2] for m in second], current)
    third = other_core(third)
    trails[0] = far(trails[0])
    trails[1] = near(trails[1])
    parts, third, trails[0], trails[1] = by_deadline(parts, third, trails[0], trails[1])
    part = parts.sum(0)
    parts = swap(copies(part, row_size), "row")
    trails[0] = other_core(trails[0])
    trails[1] = far(trails[1])
    pending = product([m[:1] for m in third], solved_0) + product([m[1:2] for m in third], solved_1)
    parts, trails[0], trails[1], pending = by_deadline(parts, trails[0], trails[1], pending)
    solved_2 = solved_of(parts)

    current = sides[2] - folded((pending + product([m[2:3] for m in third], solved_2))[0])
    parts = scattered([m[3] for m in third], current)
    trails[1] = other_core(trails[1])
    below = product([m[:trail_count] for m in trails[0]], solved_0)
    below = below + product([m[trail_count:] for m in trails[0]], solved_1)
    out = sent_out(jnp.stack([out_of(s) for s in (solved_0, solved_1, solved_2)]))
    parts, trails[1], below = by_deadline(parts, trails[1], below)
    part = parts.sum(0)
    parts = swap(copies(part, row_size), "row")
    below = below + product([m[:trail_count] for m in trails[1]], solved_2)
    parts, below, out = by_deadline(parts, below, out)
    solved_3 = solved_of(parts)
    last_out = sent_out(out_of(solved_3)[None])
    solution = jnp.concatenate([out, last_out]).transpose(0, 2, 1)

    below = folded(below + product([m[trail_count:] for m in trails[1]], solved_3))
    own_below = lax.dynamic_slice_in_dim(right_sides[step_count:], col * own_width, own_width, 2)
    trail_rest = own_below - below[:, :, :own_width]
    return (solution, trail_rest)


def solution(mesh):
    placed = (
        P(None, "row", None),
        P(None, "col", "row"),
        P(None, "row", "col"),
        P(None, "row", None, "col"),
    )
    return jax.shard_map(
        shards,
        mesh=mesh,
        in_specs=placed,
        out_specs=(P(None, "col", "row"), P(None, "row", "col")),
        check_vma=False,
    )
```

```python
import jax
import jax.numpy as jnp
from jax import lax
from jax.sharding import PartitionSpec as P

PRECISION = lax.Precision.HIGHEST


def pair_index(block_row, prior_row):
    return block_row * (block_row - 1) // 2 + prior_row


def contract(left, right, axes):
    return lax.dot_general(
        left,
        right,
        (((axes[0],), (axes[1],)), ((), ())),
        precision=PRECISION,
        preferred_element_type=jnp.float32,
    )


def swap(parts, axis, groups=None):
    return lax.all_to_all(parts, axis, 0, 0, axis_index_groups=groups, tiled=True)


def copies(part, count):
    return jnp.broadcast_to(part[None], (count,) + part.shape)


def shards(right_sides, diag_inverse, lower_blocks, trail_panel):
    step_count = diag_inverse.shape[0]
    trail_count = trail_panel.shape[0]
    local_rows = right_sides.shape[1]
    column_count = right_sides.shape[2]
    width = lower_blocks.shape[2]
    row_size = lax.axis_size("row")
    col_size = lax.axis_size("col")
    members = row_size // 2
    half = column_count // 2
    row = lax.axis_index("row")
    col = lax.axis_index("col")
    parity = row % 2
    row_groups = [[r for r in range(row_size) if r % 2 == g] for g in range(2)]
    pair_groups = [
        [(r + g) * col_size + c for g in range(2) for c in range(col_size)]
        for r in range(0, row_size, 2)
    ]

    own_diag = diag_inverse.transpose(0, 2, 1)
    got_diag = lax.ppermute(own_diag[1:], "row", [(r, r ^ 1) for r in range(row_size)])
    diag = [own_diag[0]]
    for block_row in range(1, step_count):
        own, got = own_diag[block_row], got_diag[block_row - 1]
        diag.append(
            jnp.concatenate([jnp.where(parity == 0, own, got), jnp.where(parity == 0, got, own)])
        )

    solved = []
    below = None
    for block_row in range(step_count):
        if block_row == 0:
            local_term = contract(diag[0], right_sides[0], (0, 0))
            parts = local_term.reshape(row_size, width // row_size, column_count)
            part = swap(parts, "row").sum(0)
            whole = swap(copies(part, row_size), "row").reshape(width, column_count)
        else:
            term = jnp.where(col == 0, right_sides[block_row], 0.0)
            for prior_row in range(block_row):
                block = lower_blocks[pair_index(block_row, prior_row)]
                term = term - contract(block, solved[prior_row], (1, 0))
            halves = jnp.stack([term[:, :half], term[:, half:]])[:, None]
            parts = jnp.broadcast_to(halves, (2, col_size, local_rows, half))
            parts = parts.reshape(2 * col_size, local_rows, half)
            parts = swap(parts, ("row", "col"), pair_groups)
            current = parts.reshape(2, col_size, local_rows, half).sum(1)
            local_term = contract(diag[block_row], current.reshape(2 * local_rows, half), (0, 0))
            parts = local_term.reshape(members, width // members, half)
            part = swap(parts, "row", row_groups).sum(0)
            parts = swap(copies(part, row_size), "row").reshape(members, 2, -1, half)
            whole = parts.transpose(0, 2, 1, 3).reshape(width, column_count)
        solved.append(whole)
        contrib = jnp.einsum(
            "nc,mrn->cmr", whole, trail_panel[:, :, block_row, :], precision=PRECISION
        )
        below = contrib if below is None else below + contrib

    own_width = column_count // col_size
    shared = swap(below.reshape(column_count, -1), "col")
    shared = shared.reshape(col_size, own_width, -1).sum(0)
    shared = shared.reshape(own_width, trail_count, local_rows).transpose(1, 2, 0)
    own_below = lax.dynamic_slice_in_dim(right_sides[step_count:], col * own_width, own_width, 2)
    trail_rest = own_below - shared

    out_width = column_count // row_size
    outs = [lax.dynamic_slice_in_dim(whole, row * out_width, out_width, 1) for whole in solved]
    return (jnp.stack(outs), trail_rest)


def solution(mesh):
    placed = (
        P(None, "row", None),
        P(None, "col", "row"),
        P(None, "row", "col"),
        P(None, "row", None, "col"),
    )
    return jax.shard_map(
        shards,
        mesh=mesh,
        in_specs=placed,
        out_specs=(P(None, "col", "row"), P(None, "row", "col")),
        check_vma=False,
    )
```

```python
import jax
import jax.numpy as jnp
from jax import lax
from jax.sharding import PartitionSpec as P

PRECISION = lax.Precision.HIGHEST


def pair_index(block_row, prior_row):
    return block_row * (block_row - 1) // 2 + prior_row


def contract(left, right, axes):
    return lax.dot_general(
        left,
        right,
        (((axes[0],), (axes[1],)), ((), ())),
        precision=PRECISION,
        preferred_element_type=jnp.float32,
    )


def swap(parts, axis, groups=None):
    return lax.all_to_all(parts, axis, 0, 0, axis_index_groups=groups, tiled=True)


def copies(part, count):
    return jnp.broadcast_to(part[None], (count,) + part.shape)


def shards(right_sides, diag_inverse, lower_blocks, trail_panel):
    step_count = diag_inverse.shape[0]
    trail_count = trail_panel.shape[0]
    local_rows = right_sides.shape[1]
    column_count = right_sides.shape[2]
    width = lower_blocks.shape[2]
    row_size = lax.axis_size("row")
    col_size = lax.axis_size("col")
    members = row_size // 2
    half = column_count // 2
    row = lax.axis_index("row")
    col = lax.axis_index("col")
    parity = row % 2
    row_groups = [[r for r in range(row_size) if r % 2 == g] for g in range(2)]
    pair_groups = [
        [(r + g) * col_size + c for g in range(2) for c in range(col_size)]
        for r in range(0, row_size, 2)
    ]

    own_diag = diag_inverse.transpose(0, 2, 1)

    def pair_diag(own_later):
        got = lax.ppermute(own_later, "row", [(r, r ^ 1) for r in range(row_size)])
        even = jnp.where(parity == 0, own_later, got)
        odd = jnp.where(parity == 0, got, own_later)
        return jnp.concatenate([even, odd], 1)

    trail = [
        trail_panel[:, :, j, :].reshape(trail_count * local_rows, width) for j in range(step_count)
    ]
    solved = []
    below = None
    for block_row in range(step_count):
        if block_row == 0:
            local_term = contract(own_diag[0], right_sides[0], (0, 0))
            parts = local_term.reshape(row_size, width // row_size, column_count)
            part = swap(parts, "row").sum(0)
            part, own_later = lax.optimization_barrier((part, own_diag[1:]))
            diag = pair_diag(own_later)
            whole = swap(copies(part, row_size), "row").reshape(width, column_count)
        else:
            term = jnp.where(col == 0, right_sides[block_row], 0.0)
            for prior_row in range(block_row):
                block = lower_blocks[pair_index(block_row, prior_row)]
                term = term - contract(block, solved[prior_row], (1, 0))
            halves = jnp.stack([term[:, :half], term[:, half:]])[:, None]
            parts = jnp.broadcast_to(halves, (2, col_size, local_rows, half))
            parts = parts.reshape(2 * col_size, local_rows, half)
            parts = swap(parts, ("row", "col"), pair_groups)
            current = parts.reshape(2, col_size, local_rows, half).sum(1)
            local_term = contract(diag[block_row - 1], current.reshape(2 * local_rows, half), (0, 0))
            parts = local_term.reshape(members, width // members, half)
            part = swap(parts, "row", row_groups).sum(0)
            parts = swap(copies(part, row_size), "row").reshape(members, 2, -1, half)
            whole = parts.transpose(0, 2, 1, 3).reshape(width, column_count)
        solved.append(whole)
        contrib = contract(whole, trail[block_row], (0, 1))
        below = contrib if below is None else below + contrib

    own_width = column_count // col_size
    shared = swap(below, "col")
    shared = shared.reshape(col_size, own_width, -1).sum(0)
    shared = shared.reshape(own_width, trail_count, local_rows).transpose(1, 2, 0)
    own_below = lax.dynamic_slice_in_dim(right_sides[step_count:], col * own_width, own_width, 2)
    trail_rest = own_below - shared

    out_width = column_count // row_size
    outs = [lax.dynamic_slice_in_dim(whole, row * out_width, out_width, 1) for whole in solved]
    return (jnp.stack(outs), trail_rest)


def solution(mesh):
    placed = (
        P(None, "row", None),
        P(None, "col", "row"),
        P(None, "row", "col"),
        P(None, "row", None, "col"),
    )
    return jax.shard_map(
        shards,
        mesh=mesh,
        in_specs=placed,
        out_specs=(P(None, "col", "row"), P(None, "row", "col")),
        check_vma=False,
    )
```

```python
import jax
import jax.numpy as jnp
from jax import lax
from jax.sharding import PartitionSpec as P

PRECISION = lax.Precision.HIGHEST


def contract(left, right, axes):
    return lax.dot_general(
        left,
        right,
        (((axes[0],), (axes[1],)), ((), ())),
        precision=PRECISION,
        preferred_element_type=jnp.float32,
    )


def swap(parts, axis, groups=None):
    return lax.all_to_all(parts, axis, 0, 0, axis_index_groups=groups, tiled=True)


def copies(part, count):
    return jnp.broadcast_to(part[None], (count,) + part.shape)


def by_deadline(*values):
    return lax.optimization_barrier(values)


def shards(right_sides, diag_inverse, lower_blocks, trail_panel):
    step_count = diag_inverse.shape[0]
    trail_count = trail_panel.shape[0]
    local_rows = right_sides.shape[1]
    column_count = right_sides.shape[2]
    width = lower_blocks.shape[2]
    row_size = lax.axis_size("row")
    col_size = lax.axis_size("col")
    members = row_size // 2
    half = column_count // 2
    row = lax.axis_index("row")
    col = lax.axis_index("col")
    even = row % 2 == 0
    row_groups = [[r for r in range(row_size) if r % 2 == g] for g in range(2)]
    pair_groups = [
        [(r + g) * col_size + c for g in range(2) for c in range(col_size)]
        for r in range(0, row_size, 2)
    ]

    def from_partner(value):
        return lax.ppermute(value, "row", [(r, r ^ 1) for r in range(row_size)])

    def ordered(own, got, axis):
        return jnp.concatenate([jnp.where(even, own, got), jnp.where(even, got, own)], axis)

    def half_of(value, which):
        return lax.dynamic_slice_in_dim(value, which * half, half, value.ndim - 1)

    def halves_whole(parts):
        parts = parts.reshape(members, 2, -1, half)
        return parts.transpose(0, 2, 1, 3).reshape(width, column_count)

    def scattered(matrix, current):
        parts = contract(matrix, current, (0, 0)).reshape(members, width // members, half)
        return swap(parts, "row", row_groups)

    def gathered(parts):
        return swap(copies(parts.sum(0), members), "row", row_groups)

    def gathered_whole(parts):
        return swap(copies(parts.sum(0), row_size), "row")

    def summed(update):
        return swap(copies(update, col_size), "col").sum(0)

    def own_term(block_row):
        return jnp.where(col == 0, right_sides[block_row], 0.0)

    own_diag = diag_inverse.transpose(0, 2, 1)
    trail = [
        trail_panel[:, :, j, :].reshape(trail_count * local_rows, width) for j in range(step_count)
    ]

    def below_of(whole, block_row):
        return contract(whole, trail[block_row], (0, 1))

    out_width = column_count // row_size

    def out_of(whole):
        return lax.dynamic_slice_in_dim(whole, row * out_width, out_width, 1)

    local_term = contract(own_diag[0], right_sides[0], (0, 0))
    parts = swap(local_term.reshape(row_size, width // row_size, column_count), "row")
    part, own_later = lax.optimization_barrier((parts.sum(0), own_diag[1:]))
    parts = swap(copies(part, row_size), "row")
    parts, got_later = by_deadline(parts, from_partner(own_later))
    whole_0 = parts.reshape(width, column_count)

    term = own_term(1) - contract(lower_blocks[0], whole_0, (1, 0))
    parts = jnp.stack([term[:, :half], term[:, half:]])[:, None]
    parts = jnp.broadcast_to(parts, (2, col_size, local_rows, half))
    parts = swap(parts.reshape(2 * col_size, local_rows, half), ("row", "col"), pair_groups)
    diag = ordered(own_later, got_later, 1)
    term_2 = own_term(2) - contract(lower_blocks[1], whole_0, (1, 0))
    term_3 = own_term(3) - contract(lower_blocks[3], whole_0, (1, 0))
    shared = [lower_blocks[2], lower_blocks[4], lower_blocks[5]]
    sent = shared + [half_of(term_2, row % 2 ^ 1), half_of(term_3, row % 2 ^ 1)]
    kept = jnp.concatenate(shared + [half_of(term_2, row % 2), half_of(term_3, row % 2)], 1)
    got = from_partner(jnp.concatenate(sent, 1))
    parts, diag = by_deadline(parts, diag)
    current = parts.reshape(2, col_size, local_rows, half).sum(1).reshape(2 * local_rows, half)
    parts = scattered(diag[0], current)
    parts, got = by_deadline(parts, got)
    parts = gathered(parts)
    pair = ordered(kept, got, 0)
    lower_21, lower_31, lower_32 = [pair[:, i * width : (i + 1) * width] for i in range(3)]
    term_2 = pair[:, 3 * width : 3 * width + half]
    term_3 = pair[:, 3 * width + half :]
    below = below_of(whole_0, 0)
    parts, lower_21, lower_31, lower_32, term_2, term_3, below = by_deadline(
        parts, lower_21, lower_31, lower_32, term_2, term_3, below
    )
    solved_1 = parts.reshape(width, half)

    current = summed(term_2 - contract(lower_21, solved_1, (1, 0)))
    parts = scattered(diag[1], current)
    parts, got_1 = by_deadline(parts, from_partner(solved_1))
    parts = gathered(parts)
    whole_1 = ordered(solved_1, got_1, 1)
    term_3 = term_3 - contract(lower_31, solved_1, (1, 0))
    below = below + below_of(whole_1, 1)
    parts, term_3, below = by_deadline(parts, term_3, below)
    solved_2 = parts.reshape(width, half)

    current = summed(term_3 - contract(lower_32, solved_2, (1, 0)))
    parts = scattered(diag[2], current)
    outs = [out_of(whole_0), out_of(whole_1)]
    parts, got_2, outs = by_deadline(parts, from_partner(solved_2), outs)
    parts = gathered_whole(parts)
    whole_2 = ordered(solved_2, got_2, 1)
    below = below + below_of(whole_2, 2)
    parts, below = by_deadline(parts, below)
    whole_3 = halves_whole(parts)

    below = below + below_of(whole_3, 3)
    own_width = column_count // col_size
    shared = swap(below, "col").reshape(col_size, own_width, -1).sum(0)
    shared = shared.reshape(own_width, trail_count, local_rows).transpose(1, 2, 0)
    own_below = lax.dynamic_slice_in_dim(right_sides[step_count:], col * own_width, own_width, 2)
    trail_rest = own_below - shared
    return (jnp.stack(outs + [out_of(whole_2), out_of(whole_3)]), trail_rest)


def solution(mesh):
    placed = (
        P(None, "row", None),
        P(None, "col", "row"),
        P(None, "row", "col"),
        P(None, "row", None, "col"),
    )
    return jax.shard_map(
        shards,
        mesh=mesh,
        in_specs=placed,
        out_specs=(P(None, "col", "row"), P(None, "row", "col")),
        check_vma=False,
    )
```

```python
import jax
import jax.numpy as jnp
from jax import lax
from jax.sharding import PartitionSpec as P

PRECISION = lax.Precision.HIGHEST


def contract(left, right, axes):
    return lax.dot_general(
        left,
        right,
        (((axes[0],), (axes[1],)), ((), ())),
        precision=PRECISION,
        preferred_element_type=jnp.float32,
    )


def swap(parts, axis, groups=None):
    return lax.all_to_all(parts, axis, 0, 0, axis_index_groups=groups, tiled=True)


def copies(part, count):
    return jnp.broadcast_to(part[None], (count,) + part.shape)


def by_deadline(*values):
    return lax.optimization_barrier(values)


def shards(right_sides, diag_inverse, lower_blocks, trail_panel):
    step_count = diag_inverse.shape[0]
    trail_count = trail_panel.shape[0]
    local_rows = right_sides.shape[1]
    column_count = right_sides.shape[2]
    width = lower_blocks.shape[2]
    row_size = lax.axis_size("row")
    col_size = lax.axis_size("col")
    members = row_size // 2
    half = column_count // 2
    row = lax.axis_index("row")
    col = lax.axis_index("col")
    even = row % 2 == 0
    row_groups = [[r for r in range(row_size) if r % 2 == g] for g in range(2)]
    pair_groups = [
        [(r + g) * col_size + c for g in range(2) for c in range(col_size)]
        for r in range(0, row_size, 2)
    ]

    def from_partner(value):
        return lax.ppermute(value, "row", [(r, r ^ 1) for r in range(row_size)])

    def ordered(own, got, axis):
        return jnp.concatenate([jnp.where(even, own, got), jnp.where(even, got, own)], axis)

    def half_of(value, which):
        return lax.dynamic_slice_in_dim(value, which * half, half, value.ndim - 1)

    def halves_whole(parts):
        parts = parts.reshape(members, 2, -1, half)
        return parts.transpose(0, 2, 1, 3).reshape(width, column_count)

    def scattered(matrix, current):
        parts = contract(matrix, current, (0, 0)).reshape(members, width // members, half)
        return swap(parts, "row", row_groups)

    def gathered(parts):
        return swap(copies(parts.sum(0), members), "row", row_groups)

    def gathered_whole(parts):
        return swap(copies(parts.sum(0), row_size), "row")

    def summed(update):
        return swap(copies(update, col_size), "col")

    def own_term(block_row):
        return jnp.where(col == 0, right_sides[block_row], 0.0)

    own_diag = diag_inverse.transpose(0, 2, 1)
    trail = [
        trail_panel[:, :, j, :].reshape(trail_count * local_rows, width) for j in range(step_count)
    ]

    def below_of(whole, block_row):
        return contract(whole, trail[block_row], (0, 1))

    own_width = column_count // col_size
    own_below = lax.dynamic_slice_in_dim(
        right_sides[step_count:].transpose(0, 2, 1), col * own_width, own_width, 1
    )

    out_width = column_count // row_size

    def out_of(whole):
        return lax.dynamic_slice_in_dim(whole, row * out_width, out_width, 1)

    local_term = contract(own_diag[0], right_sides[0], (0, 0))
    parts = swap(local_term.reshape(row_size, width // row_size, column_count), "row")
    own_later = jnp.concatenate([own_diag[1:], lower_blocks[2:3], lower_blocks[4:]])
    got_later = from_partner(own_later)
    parts = swap(copies(parts.sum(0), row_size), "row")
    parts, got_later = by_deadline(parts, got_later)
    pair = ordered(own_later, got_later, 1)
    diag_1, diag_2, diag_3, lower_21, lower_31, lower_32 = [pair[i] for i in range(6)]
    whole_0 = parts.reshape(width, column_count)

    term = own_term(1) - contract(lower_blocks[0], whole_0, (1, 0))
    parts = jnp.stack([term[:, :half], term[:, half:]])[:, None]
    parts = jnp.broadcast_to(parts, (2, col_size, local_rows, half))
    parts = swap(parts.reshape(2 * col_size, local_rows, half), ("row", "col"), pair_groups)
    term_2 = own_term(2) - contract(lower_blocks[1], whole_0, (1, 0))
    term_3 = own_term(3) - contract(lower_blocks[3], whole_0, (1, 0))
    terms = jnp.stack([term_2, term_3])
    got_terms = from_partner(half_of(terms, row % 2 ^ 1))
    current = parts.reshape(2, col_size, local_rows, half).sum(1).reshape(2 * local_rows, half)
    parts = scattered(diag_1, current)
    parts, got_terms = by_deadline(parts, got_terms)
    parts = gathered(parts)
    terms = ordered(half_of(terms, row % 2), got_terms, 1)
    below = below_of(whole_0, 0)
    parts, terms, below, trail = by_deadline(parts, terms, below, trail)
    term_2, term_3 = terms[0], terms[1]
    solved_1 = parts.reshape(width, half)

    parts = summed(term_2 - contract(lower_21, solved_1, (1, 0)))
    parts, got_1 = by_deadline(parts, from_partner(solved_1))
    parts = scattered(diag_2, parts.sum(0))
    parts = gathered(parts)
    whole_1 = ordered(solved_1, got_1, 1)
    term_3 = term_3 - contract(lower_31, solved_1, (1, 0))
    below = below + below_of(whole_1, 1)
    parts, term_3, below = by_deadline(parts, term_3, below)
    solved_2 = parts.reshape(width, half)

    parts = summed(term_3 - contract(lower_32, solved_2, (1, 0)))
    parts, got_2 = by_deadline(parts, from_partner(solved_2))
    parts = scattered(diag_3, parts.sum(0))
    outs = [out_of(whole_0), out_of(whole_1)]
    parts, outs = by_deadline(parts, outs)
    parts = gathered_whole(parts)
    whole_2 = ordered(solved_2, got_2, 1)
    below = below + below_of(whole_2, 2)
    parts, below = by_deadline(parts, below)
    whole_3 = halves_whole(parts)

    below = below + below_of(whole_3, 3)
    shared = swap(below, "col").reshape(col_size, own_width, -1).sum(0)
    shared = shared.reshape(own_width, trail_count, local_rows).transpose(1, 0, 2)
    trail_rest = (own_below - shared).transpose(0, 2, 1)
    return (jnp.stack(outs + [out_of(whole_2), out_of(whole_3)]), trail_rest)


def solution(mesh):
    placed = (
        P(None, "row", None),
        P(None, "col", "row"),
        P(None, "row", "col"),
        P(None, "row", None, "col"),
    )
    return jax.shard_map(
        shards,
        mesh=mesh,
        in_specs=placed,
        out_specs=(P(None, "col", "row"), P(None, "row", "col")),
        check_vma=False,
    )
```

```python
import jax
import jax.numpy as jnp
from jax import lax
from jax.sharding import PartitionSpec as P

PRECISION = lax.Precision.HIGHEST


def contract(left, right, axes):
    return lax.dot_general(
        left,
        right,
        (((axes[0],), (axes[1],)), ((), ())),
        precision=PRECISION,
        preferred_element_type=jnp.float32,
    )


def swap(parts, axis, groups=None):
    return lax.all_to_all(parts, axis, 0, 0, axis_index_groups=groups, tiled=True)


def copies(part, count):
    return jnp.broadcast_to(part[None], (count,) + part.shape)


def by_deadline(*values):
    return lax.optimization_barrier(values)


def shards(right_sides, diag_inverse, lower_blocks, trail_panel):
    step_count = diag_inverse.shape[0]
    trail_count = trail_panel.shape[0]
    local_rows = right_sides.shape[1]
    column_count = right_sides.shape[2]
    width = lower_blocks.shape[2]
    row_size = lax.axis_size("row")
    col_size = lax.axis_size("col")
    members = row_size // 2
    half = column_count // 2
    row = lax.axis_index("row")
    col = lax.axis_index("col")
    even = row % 2 == 0
    row_groups = [[r for r in range(row_size) if r % 2 == g] for g in range(2)]
    pair_groups = [
        [(r + g) * col_size + c for g in range(2) for c in range(col_size)]
        for r in range(0, row_size, 2)
    ]

    def from_partner(value):
        return lax.ppermute(value, "row", [(r, r ^ 1) for r in range(row_size)])

    def ordered(own, got, axis):
        return jnp.concatenate([jnp.where(even, own, got), jnp.where(even, got, own)], axis)

    def half_of(value, which):
        return lax.dynamic_slice_in_dim(value, which * half, half, value.ndim - 1)

    def halves_whole(parts):
        parts = parts.reshape(members, 2, -1, half)
        return parts.transpose(0, 2, 1, 3).reshape(width, column_count)

    def scattered(matrix, current):
        parts = contract(matrix, current, (0, 0)).reshape(members, width // members, half)
        return swap(parts, "row", row_groups)

    def gathered(parts):
        return swap(copies(parts.sum(0), members), "row", row_groups)

    def gathered_whole(parts):
        return swap(copies(parts.sum(0), row_size), "row")

    def summed(update):
        return swap(copies(update, col_size), "col")

    def own_term(block_row):
        return jnp.where(col == 0, right_sides[block_row], 0.0)

    own_diag = diag_inverse.transpose(0, 2, 1)
    trail = [
        trail_panel[:, :, j, :].reshape(trail_count * local_rows, width) for j in range(step_count)
    ]

    def below_of(whole, block_row):
        return contract(whole, trail[block_row], (0, 1))

    own_width = column_count // col_size
    own_below = lax.dynamic_slice_in_dim(
        right_sides[step_count:].transpose(0, 2, 1), col * own_width, own_width, 1
    )

    out_width = column_count // row_size

    def out_of(whole):
        return lax.dynamic_slice_in_dim(whole, row * out_width, out_width, 1)

    local_term = contract(own_diag[0], right_sides[0], (0, 0))
    parts = swap(local_term.reshape(row_size, width // row_size, column_count), "row")
    own_first = jnp.concatenate([own_diag[1:3], lower_blocks[2:3]])
    own_rest = jnp.concatenate([own_diag[3:], lower_blocks[4:]])
    own_rest = own_rest.reshape(-1, local_rows, width // half, half)
    own_rest = own_rest.transpose(0, 2, 1, 3).reshape(-1, half)
    parts, got_first, trail = by_deadline(parts, from_partner(own_first), trail)
    pair = ordered(own_first, got_first, 1)
    diag_1, diag_2, lower_21 = [pair[i] for i in range(3)]
    parts = swap(copies(parts.sum(0), row_size), "row")
    whole_0 = parts.reshape(width, column_count)

    term = own_term(1) - contract(lower_blocks[0], whole_0, (1, 0))
    parts = jnp.stack([term[:, :half], term[:, half:]])[:, None]
    parts = jnp.broadcast_to(parts, (2, col_size, local_rows, half))
    parts = swap(parts.reshape(2 * col_size, local_rows, half), ("row", "col"), pair_groups)
    term_2 = own_term(2) - contract(lower_blocks[1], whole_0, (1, 0))
    term_3 = own_term(3) - contract(lower_blocks[3], whole_0, (1, 0))
    terms = jnp.stack([term_2, term_3])
    got_terms = from_partner(half_of(terms, row % 2 ^ 1))
    current = parts.reshape(2, col_size, local_rows, half).sum(1).reshape(2 * local_rows, half)
    parts = scattered(diag_1, current)
    parts, got_terms = by_deadline(parts, got_terms)
    parts = gathered(parts)
    terms = ordered(half_of(terms, row % 2), got_terms, 1)
    below = below_of(whole_0, 0)
    parts, terms, below = by_deadline(parts, terms, below)
    term_2, term_3 = terms[0], terms[1]
    solved_1 = parts.reshape(width, half)

    parts = summed(term_2 - contract(lower_21, solved_1, (1, 0)))
    got = from_partner(jnp.concatenate([own_rest, solved_1]))
    parts, got = by_deadline(parts, got)
    got_rest, got_1 = got[: own_rest.shape[0]], got[own_rest.shape[0] :]
    parts = scattered(diag_2, parts.sum(0))
    parts = gathered(parts)
    own_rest, got_rest = [
        v.reshape(-1, width // half, local_rows, half)
        .transpose(0, 2, 1, 3)
        .reshape(-1, local_rows, width)
        for v in (own_rest, got_rest)
    ]
    pair = ordered(own_rest, got_rest, 1)
    diag_3, lower_31, lower_32 = [pair[i] for i in range(3)]
    whole_1 = ordered(solved_1, got_1, 1)
    term_3 = term_3 - contract(lower_31, solved_1, (1, 0))
    below = below + below_of(whole_1, 1)
    parts, term_3, below = by_deadline(parts, term_3, below)
    solved_2 = parts.reshape(width, half)

    parts = summed(term_3 - contract(lower_32, solved_2, (1, 0)))
    parts, got_2 = by_deadline(parts, from_partner(solved_2))
    parts = scattered(diag_3, parts.sum(0))
    outs = [out_of(whole_0), out_of(whole_1)]
    parts, outs = by_deadline(parts, outs)
    parts = gathered_whole(parts)
    whole_2 = ordered(solved_2, got_2, 1)
    below = below + below_of(whole_2, 2)
    parts, below = by_deadline(parts, below)
    whole_3 = halves_whole(parts)

    below = below + below_of(whole_3, 3)
    shared = swap(below, "col").reshape(col_size, own_width, -1).sum(0)
    shared = shared.reshape(own_width, trail_count, local_rows).transpose(1, 0, 2)
    trail_rest = (own_below - shared).transpose(0, 2, 1)
    return (jnp.stack(outs + [out_of(whole_2), out_of(whole_3)]), trail_rest)


def solution(mesh):
    placed = (
        P(None, "row", None),
        P(None, "col", "row"),
        P(None, "row", "col"),
        P(None, "row", None, "col"),
    )
    return jax.shard_map(
        shards,
        mesh=mesh,
        in_specs=placed,
        out_specs=(P(None, "col", "row"), P(None, "row", "col")),
        check_vma=False,
    )
```

```python
import jax
import jax.numpy as jnp
from jax import lax
from jax.sharding import PartitionSpec as P

PRECISION = lax.Precision.HIGHEST


def contract(left, right, axes):
    return lax.dot_general(
        left,
        right,
        (((axes[0],), (axes[1],)), ((), ())),
        precision=PRECISION,
        preferred_element_type=jnp.float32,
    )


def swap(parts, axis, groups=None):
    return lax.all_to_all(parts, axis, 0, 0, axis_index_groups=groups, tiled=True)


def copies(part, count):
    return jnp.broadcast_to(part[None], (count,) + part.shape)


def by_deadline(*values):
    return lax.optimization_barrier(values)


def shards(right_sides, diag_inverse, lower_blocks, trail_panel):
    step_count = diag_inverse.shape[0]
    trail_count = trail_panel.shape[0]
    local_rows = right_sides.shape[1]
    column_count = right_sides.shape[2]
    width = lower_blocks.shape[2]
    row_size = lax.axis_size("row")
    col_size = lax.axis_size("col")
    members = row_size // 2
    half = column_count // 2
    row = lax.axis_index("row")
    col = lax.axis_index("col")
    even = row % 2 == 0
    row_groups = [[r for r in range(row_size) if r % 2 == g] for g in range(2)]

    def from_partner(value):
        return lax.ppermute(value, "row", [(r, r ^ 1) for r in range(row_size)])

    def ordered(own, got, axis):
        return jnp.concatenate([jnp.where(even, own, got), jnp.where(even, got, own)], axis)

    def half_of(value, which):
        return lax.dynamic_slice_in_dim(value, which * half, half, value.ndim - 1)

    def halves_whole(parts):
        parts = parts.reshape(members, 2, -1, half)
        return parts.transpose(0, 2, 1, 3).reshape(width, column_count)

    def scattered(matrix, current):
        parts = contract(matrix, current, (0, 0)).reshape(members, width // members, half)
        return swap(parts, "row", row_groups)

    def scattered_whole(matrix, current):
        parts = contract(matrix, current, (0, 0))
        return swap(parts.reshape(row_size, width // row_size, column_count), "row")

    def gathered(parts):
        return swap(copies(parts.sum(0), members), "row", row_groups)

    def gathered_whole(parts):
        return swap(copies(parts.sum(0), row_size), "row")

    def summed(update):
        return swap(copies(update, col_size), "col")

    def own_term(block_row):
        return jnp.where(col == 0, right_sides[block_row], 0.0)

    own_diag = diag_inverse.transpose(0, 2, 1)
    trail = [
        trail_panel[:, :, j, :].reshape(trail_count * local_rows, width) for j in range(step_count)
    ]

    def below_of(whole, block_row):
        return contract(whole, trail[block_row], (0, 1))

    own_width = column_count // col_size
    own_below = lax.dynamic_slice_in_dim(
        right_sides[step_count:].transpose(0, 2, 1), col * own_width, own_width, 1
    )

    out_width = column_count // row_size

    def out_of(whole):
        return lax.dynamic_slice_in_dim(whole, row * out_width, out_width, 1)

    parts = scattered_whole(own_diag[0], right_sides[0])
    whole_0 = gathered_whole(parts).reshape(width, column_count)

    parts = summed(contract(lower_blocks[0], whole_0, (1, 0)))
    own_shared = jnp.concatenate([own_diag[2:], lower_blocks[2:3], lower_blocks[5:]])
    parts, got_shared = by_deadline(parts, from_partner(own_shared))
    parts = scattered_whole(own_diag[1], right_sides[1] - parts.sum(0))
    term_2 = own_term(2) - contract(lower_blocks[1], whole_0, (1, 0))
    parts, got_2, trail = by_deadline(parts, from_partner(half_of(term_2, row % 2 ^ 1)), trail)
    pair = ordered(own_shared, got_shared, 1)
    diag_2, diag_3, lower_21, lower_32 = [pair[i] for i in range(4)]
    term_2 = ordered(half_of(term_2, row % 2), got_2, 0)
    term_3 = own_term(3) - contract(lower_blocks[3], whole_0, (1, 0))
    parts = gathered_whole(parts)
    below = below_of(whole_0, 0)
    parts, below, term_3 = by_deadline(parts, below, term_3)
    whole_1 = parts.reshape(width, column_count)

    parts = summed(term_2 - contract(lower_21, half_of(whole_1, row % 2), (1, 0)))
    parts = scattered(diag_2, parts.sum(0))
    term_3 = term_3 - contract(lower_blocks[4], whole_1, (1, 0))
    parts, got_3 = by_deadline(parts, from_partner(half_of(term_3, row % 2 ^ 1)))
    term_3 = ordered(half_of(term_3, row % 2), got_3, 0)
    parts = gathered(parts)
    below = below + below_of(whole_1, 1)
    parts, below, term_3 = by_deadline(parts, below, term_3)
    solved_2 = parts.reshape(width, half)

    parts = summed(term_3 - contract(lower_32, solved_2, (1, 0)))
    parts, got_2 = by_deadline(parts, from_partner(solved_2))
    parts = scattered(diag_3, parts.sum(0))
    outs = [out_of(whole_0), out_of(whole_1)]
    parts, outs = by_deadline(parts, outs)
    parts = gathered_whole(parts)
    whole_2 = ordered(solved_2, got_2, 1)
    below = below + below_of(whole_2, 2)
    parts, below = by_deadline(parts, below)
    whole_3 = halves_whole(parts)

    below = below + below_of(whole_3, 3)
    shared = swap(below, "col").reshape(col_size, own_width, -1).sum(0)
    shared = shared.reshape(own_width, trail_count, local_rows).transpose(1, 0, 2)
    trail_rest = (own_below - shared).transpose(0, 2, 1)
    return (jnp.stack(outs + [out_of(whole_2), out_of(whole_3)]), trail_rest)


def solution(mesh):
    placed = (
        P(None, "row", None),
        P(None, "col", "row"),
        P(None, "row", "col"),
        P(None, "row", None, "col"),
    )
    return jax.shard_map(
        shards,
        mesh=mesh,
        in_specs=placed,
        out_specs=(P(None, "col", "row"), P(None, "row", "col")),
        check_vma=False,
    )
```

```python
import jax
import jax.numpy as jnp
from jax import lax
from jax.sharding import PartitionSpec as P

PRECISION = lax.Precision.HIGHEST


def contract(left, right, axes):
    return lax.dot_general(
        left,
        right,
        (((axes[0],), (axes[1],)), ((), ())),
        precision=PRECISION,
        preferred_element_type=jnp.float32,
    )


def swap(parts, axis, groups=None):
    return lax.all_to_all(parts, axis, 0, 0, axis_index_groups=groups, tiled=True)


def copies(part, count):
    return jnp.broadcast_to(part[None], (count,) + part.shape)


def by_deadline(*values):
    return lax.optimization_barrier(values)


def shards(right_sides, diag_inverse, lower_blocks, trail_panel):
    step_count = diag_inverse.shape[0]
    trail_count = trail_panel.shape[0]
    local_rows = right_sides.shape[1]
    column_count = right_sides.shape[2]
    width = lower_blocks.shape[2]
    row_size = lax.axis_size("row")
    col_size = lax.axis_size("col")
    members = row_size // 2
    half = column_count // 2
    row = lax.axis_index("row")
    col = lax.axis_index("col")
    even = row % 2 == 0
    row_groups = [[r for r in range(row_size) if r % 2 == g] for g in range(2)]
    pair_groups = [
        [(r + g) * col_size + c for g in range(2) for c in range(col_size)]
        for r in range(0, row_size, 2)
    ]

    def from_partner(value):
        return lax.ppermute(value, "row", [(r, r ^ 1) for r in range(row_size)])

    def ordered(own, got, axis):
        return jnp.concatenate([jnp.where(even, own, got), jnp.where(even, got, own)], axis)

    def half_of(value, which):
        return lax.dynamic_slice_in_dim(value, which * half, half, value.ndim - 1)

    def halves_whole(parts):
        parts = parts.reshape(members, 2, -1, half)
        return parts.transpose(0, 2, 1, 3).reshape(width, column_count)

    def scattered(matrix, current):
        parts = contract(matrix, current, (0, 0)).reshape(members, width // members, half)
        return swap(parts, "row", row_groups)

    def scattered_whole(matrix, current):
        parts = contract(matrix, current, (0, 0))
        return swap(parts.reshape(row_size, width // row_size, column_count), "row")

    def gathered(parts):
        return swap(copies(parts.sum(0), members), "row", row_groups)

    def gathered_whole(parts):
        return swap(copies(parts.sum(0), row_size), "row")

    def summed(update):
        return swap(copies(update, col_size), "col")

    def own_term(block_row):
        return jnp.where(col == 0, right_sides[block_row], 0.0)

    own_diag = diag_inverse.transpose(0, 2, 1)
    trail = [
        trail_panel[:, :, j, :].reshape(trail_count * local_rows, width) for j in range(step_count)
    ]

    def below_of(whole, block_row):
        return contract(whole, trail[block_row], (0, 1))

    own_width = column_count // col_size
    own_below = lax.dynamic_slice_in_dim(
        right_sides[step_count:].transpose(0, 2, 1), col * own_width, own_width, 1
    )

    out_width = column_count // row_size

    def out_of(whole):
        return lax.dynamic_slice_in_dim(whole, row * out_width, out_width, 1)

    parts = scattered_whole(own_diag[0], right_sides[0])
    whole_0 = gathered_whole(parts).reshape(width, column_count)

    own_shared = jnp.concatenate([own_diag[1:], lower_blocks[2:3], lower_blocks[5:]])
    got_shared = from_partner(own_shared)

    term = own_term(1) - contract(lower_blocks[0], whole_0, (1, 0))
    parts = jnp.stack([term[:, :half], term[:, half:]])[:, None]
    parts = jnp.broadcast_to(parts, (2, col_size, local_rows, half))
    parts = swap(parts.reshape(2 * col_size, local_rows, half), ("row", "col"), pair_groups)
    parts, got_shared = by_deadline(parts, got_shared)
    pair = ordered(own_shared, got_shared, 1)
    diag_1, diag_2, diag_3, lower_21, lower_32 = [pair[i] for i in range(5)]
    current = parts.reshape(2, col_size, local_rows, half).sum(1).reshape(2 * local_rows, half)
    parts = scattered(diag_1, current)
    term_2 = own_term(2) - contract(lower_blocks[1], whole_0, (1, 0))
    parts, got_2, trail = by_deadline(parts, from_partner(half_of(term_2, row % 2 ^ 1)), trail)
    term_2 = ordered(half_of(term_2, row % 2), got_2, 0)
    term_3 = own_term(3) - contract(lower_blocks[3], whole_0, (1, 0))
    parts = gathered(parts)
    below = below_of(whole_0, 0)
    parts, below, term_2, term_3 = by_deadline(parts, below, term_2, term_3)
    solved_1 = parts.reshape(width, half)

    parts = summed(term_2 - contract(lower_21, solved_1, (1, 0)))
    parts, got_1 = by_deadline(parts, from_partner(solved_1))
    whole_1 = ordered(solved_1, got_1, 1)
    parts = scattered(diag_2, parts.sum(0))
    term_3 = term_3 - contract(lower_blocks[4], whole_1, (1, 0))
    parts, got_3 = by_deadline(parts, from_partner(half_of(term_3, row % 2 ^ 1)))
    term_3 = ordered(half_of(term_3, row % 2), got_3, 0)
    parts = gathered(parts)
    below = below + below_of(whole_1, 1)
    parts, below, term_3 = by_deadline(parts, below, term_3)
    solved_2 = parts.reshape(width, half)

    parts = summed(term_3 - contract(lower_32, solved_2, (1, 0)))
    parts, got_2 = by_deadline(parts, from_partner(solved_2))
    parts = scattered(diag_3, parts.sum(0))
    outs = [out_of(whole_0), out_of(whole_1)]
    parts, outs = by_deadline(parts, outs)
    parts = gathered_whole(parts)
    whole_2 = ordered(solved_2, got_2, 1)
    below = below + below_of(whole_2, 2)
    parts, below = by_deadline(parts, below)
    whole_3 = halves_whole(parts)

    below = below + below_of(whole_3, 3)
    shared = swap(below, "col").reshape(col_size, own_width, -1).sum(0)
    shared = shared.reshape(own_width, trail_count, local_rows).transpose(1, 0, 2)
    trail_rest = (own_below - shared).transpose(0, 2, 1)
    return (jnp.stack(outs + [out_of(whole_2), out_of(whole_3)]), trail_rest)


def solution(mesh):
    placed = (
        P(None, "row", None),
        P(None, "col", "row"),
        P(None, "row", "col"),
        P(None, "row", None, "col"),
    )
    return jax.shard_map(
        shards,
        mesh=mesh,
        in_specs=placed,
        out_specs=(P(None, "col", "row"), P(None, "row", "col")),
        check_vma=False,
    )
```

```python
import jax
import jax.numpy as jnp
from jax import lax
from jax.sharding import PartitionSpec as P

PRECISION = lax.Precision.HIGHEST


def contract(left, right, axes):
    return lax.dot_general(
        left,
        right,
        (((axes[0],), (axes[1],)), ((), ())),
        precision=PRECISION,
        preferred_element_type=jnp.float32,
    )


def swap(parts, axis, groups=None):
    return lax.all_to_all(parts, axis, 0, 0, axis_index_groups=groups, tiled=True)


def copies(part, count):
    return jnp.broadcast_to(part[None], (count,) + part.shape)


def by_deadline(*values):
    return lax.optimization_barrier(values)


def shards(right_sides, diag_inverse, lower_blocks, trail_panel):
    step_count = diag_inverse.shape[0]
    trail_count = trail_panel.shape[0]
    local_rows = right_sides.shape[1]
    column_count = right_sides.shape[2]
    width = lower_blocks.shape[2]
    row_size = lax.axis_size("row")
    col_size = lax.axis_size("col")
    members = row_size // 2
    half = column_count // 2
    row = lax.axis_index("row")
    col = lax.axis_index("col")
    even = row % 2 == 0
    row_groups = [[r for r in range(row_size) if r % 2 == g] for g in range(2)]
    pair_groups = [
        [(r + g) * col_size + c for g in range(2) for c in range(col_size)]
        for r in range(0, row_size, 2)
    ]

    def from_partner(value):
        return lax.ppermute(value, "row", [(r, r ^ 1) for r in range(row_size)])

    def ordered(own, got, axis):
        return jnp.concatenate([jnp.where(even, own, got), jnp.where(even, got, own)], axis)

    def half_of(value, which):
        return lax.dynamic_slice_in_dim(value, which * half, half, value.ndim - 1)

    def halves_whole(parts):
        parts = parts.reshape(members, 2, -1, half)
        return parts.transpose(0, 2, 1, 3).reshape(width, column_count)

    def scattered(matrix, current):
        parts = contract(matrix, current, (0, 0)).reshape(members, width // members, half)
        return swap(parts, "row", row_groups)

    def scattered_whole(matrix, current):
        parts = contract(matrix, current, (0, 0))
        return swap(parts.reshape(row_size, width // row_size, column_count), "row")

    def gathered(parts):
        return swap(copies(parts.sum(0), members), "row", row_groups)

    def gathered_whole(parts):
        return swap(copies(parts.sum(0), row_size), "row")

    def summed(update):
        return swap(copies(update, col_size), "col")

    def own_term(block_row):
        return jnp.where(col == 0, right_sides[block_row], 0.0)

    own_diag = diag_inverse.transpose(0, 2, 1)
    def below_of(whole, block_row):
        return contract(whole, trail[block_row], (0, 1))

    own_width = column_count // col_size
    own_below = lax.dynamic_slice_in_dim(
        right_sides[step_count:].transpose(0, 2, 1), col * own_width, own_width, 1
    )

    out_width = column_count // row_size

    def out_of(whole):
        return lax.dynamic_slice_in_dim(whole, row * out_width, out_width, 1)

    parts = scattered_whole(own_diag[0], right_sides[0])
    whole_0 = gathered_whole(parts).reshape(width, column_count)

    own_shared = jnp.concatenate([own_diag[1:], lower_blocks[2:3], lower_blocks[5:]])
    got_shared = from_partner(own_shared)

    term = own_term(1) - contract(lower_blocks[0], whole_0, (1, 0))
    parts = jnp.stack([term[:, :half], term[:, half:]])[:, None]
    parts = jnp.broadcast_to(parts, (2, col_size, local_rows, half))
    parts = swap(parts.reshape(2 * col_size, local_rows, half), ("row", "col"), pair_groups)
    diag_1 = ordered(own_shared[0], got_shared[0], 0)
    parts, diag_1, trail_panel, own_shared, got_shared = by_deadline(
        parts, diag_1, trail_panel, own_shared, got_shared
    )
    pair = ordered(own_shared[1:], got_shared[1:], 1)
    diag_2, diag_3, lower_21, lower_32 = [pair[i] for i in range(4)]
    trail = [
        trail_panel[:, :, j, :].reshape(trail_count * local_rows, width) for j in range(step_count)
    ]
    current = parts.reshape(2, col_size, local_rows, half).sum(1).reshape(2 * local_rows, half)
    parts = scattered(diag_1, current)
    term_2 = own_term(2) - contract(lower_blocks[1], whole_0, (1, 0))
    parts, got_2 = by_deadline(parts, from_partner(half_of(term_2, row % 2 ^ 1)))
    term_2 = ordered(half_of(term_2, row % 2), got_2, 0)
    term_3 = own_term(3) - contract(lower_blocks[3], whole_0, (1, 0))
    parts = gathered(parts)
    below = below_of(whole_0, 0)
    parts, below, term_2, term_3, lower_21, trail = by_deadline(
        parts, below, term_2, term_3, lower_21, trail
    )
    solved_1 = parts.reshape(width, half)

    parts = summed(term_2 - contract(lower_21, solved_1, (1, 0)))
    parts, got_1 = by_deadline(parts, from_partner(solved_1))
    whole_1 = ordered(solved_1, got_1, 1)
    parts = scattered(diag_2, parts.sum(0))
    term_3 = term_3 - contract(lower_blocks[4], whole_1, (1, 0))
    parts, got_3 = by_deadline(parts, from_partner(half_of(term_3, row % 2 ^ 1)))
    term_3 = ordered(half_of(term_3, row % 2), got_3, 0)
    parts = gathered(parts)
    below = below + below_of(whole_1, 1)
    parts, below, term_3 = by_deadline(parts, below, term_3)
    solved_2 = parts.reshape(width, half)

    parts = summed(term_3 - contract(lower_32, solved_2, (1, 0)))
    parts, got_2 = by_deadline(parts, from_partner(solved_2))
    parts = scattered(diag_3, parts.sum(0))
    outs = [out_of(whole_0), out_of(whole_1)]
    parts, outs = by_deadline(parts, outs)
    parts = gathered_whole(parts)
    whole_2 = ordered(solved_2, got_2, 1)
    below = below + below_of(whole_2, 2)
    parts, below = by_deadline(parts, below)
    whole_3 = halves_whole(parts)

    below = below + below_of(whole_3, 3)
    shared = swap(below, "col").reshape(col_size, own_width, -1).sum(0)
    shared = shared.reshape(own_width, trail_count, local_rows).transpose(1, 0, 2)
    trail_rest = (own_below - shared).transpose(0, 2, 1)
    return (jnp.stack(outs + [out_of(whole_2), out_of(whole_3)]), trail_rest)


def solution(mesh):
    placed = (
        P(None, "row", None),
        P(None, "col", "row"),
        P(None, "row", "col"),
        P(None, "row", None, "col"),
    )
    return jax.shard_map(
        shards,
        mesh=mesh,
        in_specs=placed,
        out_specs=(P(None, "col", "row"), P(None, "row", "col")),
        check_vma=False,
    )
```

```python
import jax
import jax.numpy as jnp
from jax import lax
from jax.sharding import PartitionSpec as P

PRECISION = lax.Precision.HIGHEST


def contract(left, right, axes):
    return lax.dot_general(
        left,
        right,
        (((axes[0],), (axes[1],)), ((), ())),
        precision=PRECISION,
        preferred_element_type=jnp.float32,
    )


def swap(parts, axis, groups=None):
    return lax.all_to_all(parts, axis, 0, 0, axis_index_groups=groups, tiled=True)


def copies(part, count):
    return jnp.broadcast_to(part[None], (count,) + part.shape)


def by_deadline(*values):
    return lax.optimization_barrier(values)


def shards(right_sides, diag_inverse, lower_blocks, trail_panel):
    step_count = diag_inverse.shape[0]
    trail_count = trail_panel.shape[0]
    local_rows = right_sides.shape[1]
    column_count = right_sides.shape[2]
    width = lower_blocks.shape[2]
    row_size = lax.axis_size("row")
    col_size = lax.axis_size("col")
    members = row_size // 2
    half = column_count // 2
    row = lax.axis_index("row")
    col = lax.axis_index("col")
    even = row % 2 == 0
    row_groups = [[r for r in range(row_size) if r % 2 == g] for g in range(2)]
    pair_groups = [
        [(r + g) * col_size + c for g in range(2) for c in range(col_size)]
        for r in range(0, row_size, 2)
    ]

    def from_partner(value):
        return lax.ppermute(value, "row", [(r, r ^ 1) for r in range(row_size)])

    def ordered(own, got, axis):
        return jnp.concatenate([jnp.where(even, own, got), jnp.where(even, got, own)], axis)

    def half_of(value, which):
        return lax.dynamic_slice_in_dim(value, which * half, half, value.ndim - 1)

    def halves_whole(parts):
        parts = parts.reshape(members, 2, -1, half)
        return parts.transpose(0, 2, 1, 3).reshape(width, column_count)

    def scattered(matrix, current):
        parts = contract(matrix, current, (0, 0)).reshape(members, width // members, half)
        return swap(parts, "row", row_groups)

    def scattered_whole(matrix, current):
        parts = contract(matrix, current, (0, 0))
        return swap(parts.reshape(row_size, width // row_size, column_count), "row")

    def gathered(parts):
        return swap(copies(parts.sum(0), members), "row", row_groups)

    def gathered_whole(parts):
        return swap(copies(parts.sum(0), row_size), "row")

    def summed(update):
        return swap(copies(update, col_size), "col")

    def own_term(block_row):
        return jnp.where(col == 0, right_sides[block_row], 0.0)

    own_diag = diag_inverse.transpose(0, 2, 1)
    trail = [
        trail_panel[:, :, j, :].reshape(trail_count * local_rows, width) for j in range(step_count)
    ]

    def below_of(whole, block_row):
        return contract(whole, trail[block_row], (0, 1))

    own_width = column_count // col_size
    own_below = lax.dynamic_slice_in_dim(
        right_sides[step_count:].transpose(0, 2, 1), col * own_width, own_width, 1
    )

    out_width = column_count // row_size

    def out_of(whole):
        return lax.dynamic_slice_in_dim(whole, row * out_width, out_width, 1)

    parts = scattered_whole(own_diag[0], right_sides[0])
    whole_0 = gathered_whole(parts).reshape(width, column_count)

    own_shared = jnp.concatenate([own_diag[1:], lower_blocks[2:3], lower_blocks[5:]])
    got_shared = from_partner(own_shared)

    term = own_term(1) - contract(lower_blocks[0], whole_0, (1, 0))
    parts = jnp.stack([term[:, :half], term[:, half:]])[:, None]
    parts = jnp.broadcast_to(parts, (2, col_size, local_rows, half))
    parts = swap(parts.reshape(2 * col_size, local_rows, half), ("row", "col"), pair_groups)
    diag_1 = ordered(own_shared[0], got_shared[0], 0)
    parts, diag_1, whole_0 = by_deadline(parts, diag_1, whole_0)
    pair = ordered(own_shared[1:], got_shared[1:], 1)
    diag_2, diag_3, lower_21, lower_32 = [pair[i] for i in range(4)]
    current = parts.reshape(2, col_size, local_rows, half).sum(1).reshape(2 * local_rows, half)
    parts = scattered(diag_1, current)
    term_2 = own_term(2) - contract(lower_blocks[1], whole_0, (1, 0))
    parts, got_2 = by_deadline(parts, from_partner(half_of(term_2, row % 2 ^ 1)))
    term_2 = ordered(half_of(term_2, row % 2), got_2, 0)
    term_3 = own_term(3) - contract(lower_blocks[3], whole_0, (1, 0))
    parts = gathered(parts)
    parts, term_2, term_3 = by_deadline(parts, term_2, term_3)
    solved_1 = parts.reshape(width, half)

    parts = summed(term_2 - contract(lower_21, solved_1, (1, 0)))
    parts, got_1 = by_deadline(parts, from_partner(solved_1))
    whole_1 = ordered(solved_1, got_1, 1)
    parts = scattered(diag_2, parts.sum(0))
    term_3 = term_3 - contract(lower_blocks[4], whole_1, (1, 0))
    parts, got_3 = by_deadline(parts, from_partner(half_of(term_3, row % 2 ^ 1)))
    term_3 = ordered(half_of(term_3, row % 2), got_3, 0)
    parts = gathered(parts)
    below = below_of(whole_0, 0)
    parts, below, term_3 = by_deadline(parts, below, term_3)
    solved_2 = parts.reshape(width, half)

    parts = summed(term_3 - contract(lower_32, solved_2, (1, 0)))
    parts, got_2 = by_deadline(parts, from_partner(solved_2))
    parts = scattered(diag_3, parts.sum(0))
    outs = [out_of(whole_0), out_of(whole_1)]
    below = below + below_of(whole_1, 1)
    parts, outs, below = by_deadline(parts, outs, below)
    parts = gathered_whole(parts)
    whole_2 = ordered(solved_2, got_2, 1)
    below = below + below_of(whole_2, 2)
    parts, below = by_deadline(parts, below)
    whole_3 = halves_whole(parts)

    below = below + below_of(whole_3, 3)
    shared = swap(below, "col").reshape(col_size, own_width, -1).sum(0)
    shared = shared.reshape(own_width, trail_count, local_rows).transpose(1, 0, 2)
    trail_rest = (own_below - shared).transpose(0, 2, 1)
    return (jnp.stack(outs + [out_of(whole_2), out_of(whole_3)]), trail_rest)


def solution(mesh):
    placed = (
        P(None, "row", None),
        P(None, "col", "row"),
        P(None, "row", "col"),
        P(None, "row", None, "col"),
    )
    return jax.shard_map(
        shards,
        mesh=mesh,
        in_specs=placed,
        out_specs=(P(None, "col", "row"), P(None, "row", "col")),
        check_vma=False,
    )
```

```python
import jax
import jax.numpy as jnp
from jax import lax
from jax.sharding import PartitionSpec as P

PRECISION = lax.Precision.HIGHEST


def contract(left, right, axes):
    return lax.dot_general(
        left,
        right,
        (((axes[0],), (axes[1],)), ((), ())),
        precision=PRECISION,
        preferred_element_type=jnp.float32,
    )


def swap(parts, axis, groups=None):
    return lax.all_to_all(parts, axis, 0, 0, axis_index_groups=groups, tiled=True)


def copies(part, count):
    return jnp.broadcast_to(part[None], (count,) + part.shape)


def by_deadline(*values):
    return lax.optimization_barrier(values)


def shards(right_sides, diag_inverse, lower_blocks, trail_panel):
    step_count = diag_inverse.shape[0]
    trail_count = trail_panel.shape[0]
    local_rows = right_sides.shape[1]
    column_count = right_sides.shape[2]
    width = lower_blocks.shape[2]
    row_size = lax.axis_size("row")
    col_size = lax.axis_size("col")
    members = row_size // 2
    half = column_count // 2
    row = lax.axis_index("row")
    col = lax.axis_index("col")
    even = row % 2 == 0
    row_groups = [[r for r in range(row_size) if r % 2 == g] for g in range(2)]
    pair_groups = [
        [(r + g) * col_size + c for g in range(2) for c in range(col_size)]
        for r in range(0, row_size, 2)
    ]

    def from_partner(value):
        return lax.ppermute(value, "row", [(r, r ^ 1) for r in range(row_size)])

    def ordered(own, got, axis):
        return jnp.concatenate([jnp.where(even, own, got), jnp.where(even, got, own)], axis)

    def half_of(value, which):
        return lax.dynamic_slice_in_dim(value, which * half, half, value.ndim - 1)

    def halves_whole(parts):
        parts = parts.reshape(members, 2, -1, half)
        return parts.transpose(0, 2, 1, 3).reshape(width, column_count)

    def scattered(value):
        return swap(value.reshape(members, width // members, half), "row", row_groups)

    def scattered_whole(matrix, current):
        parts = contract(matrix, current, (0, 0))
        return swap(parts.reshape(row_size, width // row_size, column_count), "row")

    def gathered(parts):
        return swap(copies(parts.sum(0), members), "row", row_groups)

    def gathered_whole(parts):
        return swap(copies(parts.sum(0), row_size), "row")

    def summed(update):
        return swap(copies(update, col_size), "col")

    def own_term(block_row):
        return jnp.where(col == 0, right_sides[block_row], 0.0)

    own_diag = diag_inverse.transpose(0, 2, 1)
    trail = [
        trail_panel[:, :, j, :].reshape(trail_count * local_rows, width) for j in range(step_count)
    ]

    def below_of(whole, block_row):
        return contract(whole, trail[block_row], (0, 1))

    own_width = column_count // col_size
    own_below = lax.dynamic_slice_in_dim(
        right_sides[step_count:].transpose(0, 2, 1), col * own_width, own_width, 1
    )

    out_width = column_count // row_size

    def out_of(whole):
        return lax.dynamic_slice_in_dim(whole, row * out_width, out_width, 1)

    parts = scattered_whole(own_diag[0], right_sides[0])
    parts, trail = by_deadline(gathered_whole(parts), trail)
    whole_0 = parts.reshape(width, column_count)

    own_shared = jnp.concatenate([own_diag[1:], lower_blocks[2:3], lower_blocks[4:]])
    got_shared = from_partner(own_shared)

    term = own_term(1) - contract(lower_blocks[0], whole_0, (1, 0))
    parts = jnp.stack([term[:, :half], term[:, half:]])[:, None]
    parts = jnp.broadcast_to(parts, (2, col_size, local_rows, half))
    parts = swap(parts.reshape(2 * col_size, local_rows, half), ("row", "col"), pair_groups)
    diag_1 = ordered(own_shared[0], got_shared[0], 0)
    parts, diag_1, whole_0 = by_deadline(parts, diag_1, whole_0)
    pair = ordered(own_shared[1:], got_shared[1:], 1)
    diag_2, diag_3, lower_21, lower_31, lower_32 = [pair[i] for i in range(5)]
    current = parts.reshape(2, col_size, local_rows, half).sum(1).reshape(2 * local_rows, half)
    parts = scattered(contract(diag_1, current, (0, 0)))
    terms = jnp.stack(
        [
            own_term(2) - contract(lower_blocks[1], whole_0, (1, 0)),
            own_term(3) - contract(lower_blocks[3], whole_0, (1, 0)),
        ]
    )
    parts, got_terms = by_deadline(parts, from_partner(half_of(terms, row % 2 ^ 1)))
    terms = ordered(half_of(terms, row % 2), got_terms, 1)
    parts = gathered(parts)
    below = below_of(whole_0, 0)
    parts, terms, below = by_deadline(parts, terms, below)
    solved_1 = parts.reshape(width, half)

    parts = summed(terms[0] - contract(lower_21, solved_1, (1, 0)))
    parts, got_1 = by_deadline(parts, from_partner(solved_1))
    local_term = contract(diag_2, parts.sum(0), (0, 0))
    local_term, got_1, solved_1 = by_deadline(local_term, got_1, solved_1)
    parts = scattered(local_term)
    term_3 = terms[1] - contract(lower_31, solved_1, (1, 0))
    whole_1 = ordered(solved_1, got_1, 1)
    parts, term_3, whole_1 = by_deadline(parts, term_3, whole_1)
    parts = gathered(parts)
    below = below + below_of(whole_1, 1)
    parts, below = by_deadline(parts, below)
    solved_2 = parts.reshape(width, half)

    parts = summed(term_3 - contract(lower_32, solved_2, (1, 0)))
    parts, got_2 = by_deadline(parts, from_partner(solved_2))
    local_term = contract(diag_3, parts.sum(0), (0, 0))
    local_term, got_2, solved_2 = by_deadline(local_term, got_2, solved_2)
    parts = scattered(local_term)
    outs = [out_of(whole_0), out_of(whole_1)]
    parts, outs = by_deadline(parts, outs)
    parts = gathered_whole(parts)
    whole_2 = ordered(solved_2, got_2, 1)
    below = below + below_of(whole_2, 2)
    parts, below = by_deadline(parts, below)
    whole_3 = halves_whole(parts)

    below = below + below_of(whole_3, 3)
    shared = swap(below, "col").reshape(col_size, own_width, -1).sum(0)
    shared = shared.reshape(own_width, trail_count, local_rows).transpose(1, 0, 2)
    trail_rest = (own_below - shared).transpose(0, 2, 1)
    return (jnp.stack(outs + [out_of(whole_2), out_of(whole_3)]), trail_rest)


def solution(mesh):
    placed = (
        P(None, "row", None),
        P(None, "col", "row"),
        P(None, "row", "col"),
        P(None, "row", None, "col"),
    )
    return jax.shard_map(
        shards,
        mesh=mesh,
        in_specs=placed,
        out_specs=(P(None, "col", "row"), P(None, "row", "col")),
        check_vma=False,
    )
```

```python
import jax
import jax.numpy as jnp
from jax import lax
from jax.sharding import PartitionSpec as P

PRECISION = lax.Precision.HIGHEST


def contract(left, right, axes):
    return lax.dot_general(
        left,
        right,
        (((axes[0],), (axes[1],)), ((), ())),
        precision=PRECISION,
        preferred_element_type=jnp.float32,
    )


def swap(parts, axis, groups=None):
    return lax.all_to_all(parts, axis, 0, 0, axis_index_groups=groups, tiled=True)


def copies(part, count):
    return jnp.broadcast_to(part[None], (count,) + part.shape)


def by_deadline(*values):
    return lax.optimization_barrier(values)


def shards(right_sides, diag_inverse, lower_blocks, trail_panel):
    step_count = diag_inverse.shape[0]
    trail_count = trail_panel.shape[0]
    local_rows = right_sides.shape[1]
    column_count = right_sides.shape[2]
    width = lower_blocks.shape[2]
    row_size = lax.axis_size("row")
    col_size = lax.axis_size("col")
    members = row_size // 2
    half = column_count // 2
    row = lax.axis_index("row")
    col = lax.axis_index("col")
    even = row % 2 == 0
    row_groups = [[r for r in range(row_size) if r % 2 == g] for g in range(2)]
    pair_groups = [
        [(r + g) * col_size + c for g in range(2) for c in range(col_size)]
        for r in range(0, row_size, 2)
    ]

    def from_partner(value):
        return lax.ppermute(value, "row", [(r, r ^ 1) for r in range(row_size)])

    def ordered(own, got, axis):
        return jnp.concatenate([jnp.where(even, own, got), jnp.where(even, got, own)], axis)

    def half_of(value, which):
        return lax.dynamic_slice_in_dim(value, which * half, half, value.ndim - 1)

    def halves_whole(parts):
        parts = parts.reshape(members, 2, -1, half)
        return parts.transpose(0, 2, 1, 3).reshape(width, column_count)

    def scattered(matrix, current):
        parts = contract(matrix, current, (0, 0)).reshape(members, width // members, half)
        return swap(parts, "row", row_groups)

    def scattered_whole(matrix, current):
        parts = contract(matrix, current, (0, 0))
        return swap(parts.reshape(row_size, width // row_size, column_count), "row")

    def gathered(parts):
        return swap(copies(parts.sum(0), members), "row", row_groups)

    def gathered_whole(parts):
        return swap(copies(parts.sum(0), row_size), "row")

    def summed(update):
        return swap(copies(update, col_size), "col")

    def own_term(block_row):
        return jnp.where(col == 0, right_sides[block_row], 0.0)

    own_diag = diag_inverse.transpose(0, 2, 1)
    trail = [
        trail_panel[:, :, j, :].reshape(trail_count * local_rows, width) for j in range(step_count)
    ]

    def below_of(whole, block_row):
        return contract(whole, trail[block_row], (0, 1))

    own_width = column_count // col_size
    own_below = lax.dynamic_slice_in_dim(
        right_sides[step_count:].transpose(0, 2, 1), col * own_width, own_width, 1
    )

    out_width = column_count // row_size

    def out_of(whole):
        return lax.dynamic_slice_in_dim(whole, row * out_width, out_width, 1)

    parts = scattered_whole(own_diag[0], right_sides[0])
    parts, trail = by_deadline(gathered_whole(parts), trail)
    whole_0 = parts.reshape(width, column_count)

    own_shared = jnp.concatenate([own_diag[1:], lower_blocks[2:3], lower_blocks[5:]])
    got_shared = from_partner(own_shared)

    term = own_term(1) - contract(lower_blocks[0], whole_0, (1, 0))
    parts = jnp.stack([term[:, :half], term[:, half:]])[:, None]
    parts = jnp.broadcast_to(parts, (2, col_size, local_rows, half))
    parts = swap(parts.reshape(2 * col_size, local_rows, half), ("row", "col"), pair_groups)
    diag_1 = ordered(own_shared[0], got_shared[0], 0)
    parts, diag_1, whole_0 = by_deadline(parts, diag_1, whole_0)
    pair = ordered(own_shared[1:], got_shared[1:], 1)
    diag_2, diag_3, lower_21, lower_32 = [pair[i] for i in range(4)]
    current = parts.reshape(2, col_size, local_rows, half).sum(1).reshape(2 * local_rows, half)
    parts = scattered(diag_1, current)
    term_2 = own_term(2) - contract(lower_blocks[1], whole_0, (1, 0))
    parts, got_2 = by_deadline(parts, from_partner(half_of(term_2, row % 2 ^ 1)))
    term_2 = ordered(half_of(term_2, row % 2), got_2, 0)
    term_3 = own_term(3) - contract(lower_blocks[3], whole_0, (1, 0))
    parts = gathered(parts)
    below = below_of(whole_0, 0)
    parts, term_2, term_3, below = by_deadline(parts, term_2, term_3, below)
    solved_1 = parts.reshape(width, half)

    parts = summed(term_2 - contract(lower_21, solved_1, (1, 0)))
    parts, got_1 = by_deadline(parts, from_partner(solved_1))
    whole_1 = ordered(solved_1, got_1, 1)
    parts = scattered(diag_2, parts.sum(0))
    term_3 = term_3 - contract(lower_blocks[4], whole_1, (1, 0))
    parts, got_3 = by_deadline(parts, from_partner(half_of(term_3, row % 2 ^ 1)))
    term_3 = ordered(half_of(term_3, row % 2), got_3, 0)
    parts = gathered(parts)
    below = below + below_of(whole_1, 1)
    parts, below, term_3 = by_deadline(parts, below, term_3)
    solved_2 = parts.reshape(width, half)

    parts = summed(term_3 - contract(lower_32, solved_2, (1, 0)))
    parts, got_2 = by_deadline(parts, from_partner(solved_2))
    parts = scattered(diag_3, parts.sum(0))
    outs = [out_of(whole_0), out_of(whole_1)]
    parts, outs = by_deadline(parts, outs)
    parts = gathered_whole(parts)
    whole_2 = ordered(solved_2, got_2, 1)
    below = below + below_of(whole_2, 2)
    parts, below = by_deadline(parts, below)
    whole_3 = halves_whole(parts)

    below = below + below_of(whole_3, 3)
    shared = swap(below, "col").reshape(col_size, own_width, -1).sum(0)
    shared = shared.reshape(own_width, trail_count, local_rows).transpose(1, 0, 2)
    trail_rest = (own_below - shared).transpose(0, 2, 1)
    return (jnp.stack(outs + [out_of(whole_2), out_of(whole_3)]), trail_rest)


def solution(mesh):
    placed = (
        P(None, "row", None),
        P(None, "col", "row"),
        P(None, "row", "col"),
        P(None, "row", None, "col"),
    )
    return jax.shard_map(
        shards,
        mesh=mesh,
        in_specs=placed,
        out_specs=(P(None, "col", "row"), P(None, "row", "col")),
        check_vma=False,
    )
```

```python
import jax
import jax.numpy as jnp
from jax import lax
from jax.sharding import PartitionSpec as P

PRECISION = lax.Precision.HIGHEST


def contract(left, right, axes):
    return lax.dot_general(
        left,
        right,
        (((axes[0],), (axes[1],)), ((), ())),
        precision=PRECISION,
        preferred_element_type=jnp.float32,
    )


def swap(parts, axis, groups=None):
    return lax.all_to_all(parts, axis, 0, 0, axis_index_groups=groups, tiled=True)


def copies(part, count):
    return jnp.broadcast_to(part[None], (count,) + part.shape)


def by_deadline(*values):
    return lax.optimization_barrier(values)


def shards(right_sides, diag_inverse, lower_blocks, trail_panel):
    step_count = diag_inverse.shape[0]
    trail_count = trail_panel.shape[0]
    local_rows = right_sides.shape[1]
    column_count = right_sides.shape[2]
    width = lower_blocks.shape[2]
    row_size = lax.axis_size("row")
    col_size = lax.axis_size("col")
    members = row_size // 2
    half = column_count // 2
    row = lax.axis_index("row")
    col = lax.axis_index("col")
    even = row % 2 == 0
    row_groups = [[r for r in range(row_size) if r % 2 == g] for g in range(2)]

    def from_partner(value):
        return lax.ppermute(value, "row", [(r, r ^ 1) for r in range(row_size)])

    def ordered(own, got, axis):
        return jnp.concatenate([jnp.where(even, own, got), jnp.where(even, got, own)], axis)

    def half_of(value, which):
        return lax.dynamic_slice_in_dim(value, which * half, half, value.ndim - 1)

    def halves_whole(parts):
        parts = parts.reshape(members, 2, -1, half)
        return parts.transpose(0, 2, 1, 3).reshape(width, column_count)

    def scattered(matrix, current):
        parts = contract(matrix, current, (0, 0)).reshape(members, width // members, half)
        return swap(parts, "row", row_groups)

    def scattered_whole(matrix, current):
        parts = contract(matrix, current, (0, 0))
        return swap(parts.reshape(row_size, width // row_size, column_count), "row")

    def gathered(parts):
        return swap(copies(parts.sum(0), members), "row", row_groups)

    def gathered_whole(parts):
        return swap(copies(parts.sum(0), row_size), "row")

    def summed(update):
        return swap(copies(update, col_size), "col")

    def own_term(block_row):
        return jnp.where(col == 0, right_sides[block_row], 0.0)

    own_diag = diag_inverse.transpose(0, 2, 1)
    trail = [
        trail_panel[:, :, j, :].reshape(trail_count * local_rows, width) for j in range(step_count)
    ]

    def below_of(whole, block_row):
        return contract(whole, trail[block_row], (0, 1))

    own_width = column_count // col_size
    own_below = lax.dynamic_slice_in_dim(
        right_sides[step_count:].transpose(0, 2, 1), col * own_width, own_width, 1
    )

    out_width = column_count // row_size

    def out_of(whole):
        return lax.dynamic_slice_in_dim(whole, row * out_width, out_width, 1)

    parts = scattered_whole(own_diag[0], right_sides[0])
    part = parts.sum(0)
    part = jnp.stack([part[:, :half], part[:, half:]])
    parts = swap(copies(part, members).reshape(row_size, -1, half), "row")
    own_first = lower_blocks[0]
    got_first = from_partner(
        jnp.concatenate([own_first, half_of(right_sides[1], row % 2 ^ 1)], 1)
    )
    lower_10 = ordered(own_first, got_first[:, :width], 0)
    side_1 = ordered(half_of(right_sides[1], row % 2), got_first[:, width:], 0)
    parts, trail, lower_10, side_1 = by_deadline(parts, trail, lower_10, side_1)
    solved_0 = parts.reshape(width, half)
    own_shared = jnp.concatenate([own_diag[1:], lower_blocks[2:3], lower_blocks[5:]])
    got_shared = from_partner(own_shared)

    parts = summed(contract(lower_10, solved_0, (1, 0)))
    diag_1 = ordered(own_shared[0], got_shared[0], 0)
    parts, diag_1, got_0 = by_deadline(parts, diag_1, from_partner(solved_0))
    whole_0 = ordered(solved_0, got_0, 1)
    pair = ordered(own_shared[1:], got_shared[1:], 1)
    diag_2, diag_3, lower_21, lower_32 = [pair[i] for i in range(4)]
    current = side_1 - parts.sum(0)
    parts = scattered(diag_1, current)
    term_2 = own_term(2) - contract(lower_blocks[1], whole_0, (1, 0))
    parts, got_2 = by_deadline(parts, from_partner(half_of(term_2, row % 2 ^ 1)))
    term_2 = ordered(half_of(term_2, row % 2), got_2, 0)
    term_3 = own_term(3) - contract(lower_blocks[3], whole_0, (1, 0))
    parts = gathered(parts)
    below = below_of(whole_0, 0)
    parts, term_2, term_3, below = by_deadline(parts, term_2, term_3, below)
    solved_1 = parts.reshape(width, half)

    parts = summed(term_2 - contract(lower_21, solved_1, (1, 0)))
    parts, got_1 = by_deadline(parts, from_partner(solved_1))
    whole_1 = ordered(solved_1, got_1, 1)
    parts = scattered(diag_2, parts.sum(0))
    term_3 = term_3 - contract(lower_blocks[4], whole_1, (1, 0))
    parts, got_3 = by_deadline(parts, from_partner(half_of(term_3, row % 2 ^ 1)))
    term_3 = ordered(half_of(term_3, row % 2), got_3, 0)
    parts = gathered(parts)
    below = below + below_of(whole_1, 1)
    parts, below, term_3 = by_deadline(parts, below, term_3)
    solved_2 = parts.reshape(width, half)

    parts = summed(term_3 - contract(lower_32, solved_2, (1, 0)))
    parts, got_2 = by_deadline(parts, from_partner(solved_2))
    parts = scattered(diag_3, parts.sum(0))
    outs = [out_of(whole_0), out_of(whole_1)]
    parts, outs = by_deadline(parts, outs)
    parts = gathered_whole(parts)
    whole_2 = ordered(solved_2, got_2, 1)
    below = below + below_of(whole_2, 2)
    parts, below = by_deadline(parts, below)
    whole_3 = halves_whole(parts)

    below = below + below_of(whole_3, 3)
    shared = swap(below, "col").reshape(col_size, own_width, -1).sum(0)
    shared = shared.reshape(own_width, trail_count, local_rows).transpose(1, 0, 2)
    trail_rest = (own_below - shared).transpose(0, 2, 1)
    return (jnp.stack(outs + [out_of(whole_2), out_of(whole_3)]), trail_rest)


def solution(mesh):
    placed = (
        P(None, "row", None),
        P(None, "col", "row"),
        P(None, "row", "col"),
        P(None, "row", None, "col"),
    )
    return jax.shard_map(
        shards,
        mesh=mesh,
        in_specs=placed,
        out_specs=(P(None, "col", "row"), P(None, "row", "col")),
        check_vma=False,
    )
```

```python
import jax
import jax.numpy as jnp
from jax import lax
from jax.sharding import PartitionSpec as P

PRECISION = lax.Precision.HIGHEST


def contract(left, right, axes):
    return lax.dot_general(
        left,
        right,
        (((axes[0],), (axes[1],)), ((), ())),
        precision=PRECISION,
        preferred_element_type=jnp.float32,
    )


def swap(parts, axis, groups=None):
    return lax.all_to_all(parts, axis, 0, 0, axis_index_groups=groups, tiled=True)


def copies(part, count):
    return jnp.broadcast_to(part[None], (count,) + part.shape)


def by_deadline(*values):
    return lax.optimization_barrier(values)


def shards(right_sides, diag_inverse, lower_blocks, trail_panel):
    step_count = diag_inverse.shape[0]
    trail_count = trail_panel.shape[0]
    local_rows = right_sides.shape[1]
    column_count = right_sides.shape[2]
    width = lower_blocks.shape[2]
    row_size = lax.axis_size("row")
    col_size = lax.axis_size("col")
    members = row_size // 2
    half = column_count // 2
    row = lax.axis_index("row")
    col = lax.axis_index("col")
    even = row % 2 == 0
    row_groups = [[r for r in range(row_size) if r % 2 == g] for g in range(2)]

    def from_partner(value):
        return lax.ppermute(value, "row", [(r, r ^ 1) for r in range(row_size)])

    def ordered(own, got, axis):
        return jnp.concatenate([jnp.where(even, own, got), jnp.where(even, got, own)], axis)

    def half_of(value, which):
        return lax.dynamic_slice_in_dim(value, which * half, half, value.ndim - 1)

    def halves_whole(parts):
        parts = parts.reshape(members, 2, -1, half)
        return parts.transpose(0, 2, 1, 3).reshape(width, column_count)

    def scattered(matrix, current):
        parts = contract(matrix, current, (0, 0)).reshape(members, width // members, half)
        return swap(parts, "row", row_groups)

    def scattered_whole(matrix, current):
        parts = contract(matrix, current, (0, 0))
        return swap(parts.reshape(row_size, width // row_size, column_count), "row")

    def gathered(parts):
        return swap(copies(parts.sum(0), members), "row", row_groups)

    def gathered_whole(parts):
        return swap(copies(parts.sum(0), row_size), "row")

    def summed(update):
        return swap(copies(update, col_size), "col")

    def own_term(block_row):
        return jnp.where(col == 0, right_sides[block_row], 0.0)

    own_diag = diag_inverse.transpose(0, 2, 1)
    trail = [
        trail_panel[:, :, j, :].reshape(trail_count * local_rows, width) for j in range(step_count)
    ]

    def below_of(whole, block_row):
        return contract(whole, trail[block_row], (0, 1))

    own_width = column_count // col_size
    own_below = lax.dynamic_slice_in_dim(
        right_sides[step_count:].transpose(0, 2, 1), col * own_width, own_width, 1
    )

    out_width = column_count // row_size

    def out_of(whole):
        return lax.dynamic_slice_in_dim(whole, row * out_width, out_width, 1)

    parts = scattered_whole(own_diag[0], right_sides[0])
    sent_first = jnp.concatenate([lower_blocks[0], half_of(right_sides[1], row % 2 ^ 1)], 1)
    part, sent_first = by_deadline(parts.sum(0), sent_first)
    part = jnp.stack([part[:, :half], part[:, half:]])
    parts = swap(copies(part, members).reshape(row_size, -1, half), "row")
    got_first = from_partner(sent_first)
    own_shared = jnp.concatenate([own_diag[1:], lower_blocks[2:3], lower_blocks[5:]])
    got_first, own_shared = by_deadline(got_first, own_shared)
    got_shared = from_partner(own_shared)
    lower_10 = ordered(lower_blocks[0], got_first[:, :width], 0)
    side_1 = ordered(half_of(right_sides[1], row % 2), got_first[:, width:], 0)
    parts, trail, lower_10, side_1 = by_deadline(parts, trail, lower_10, side_1)
    solved_0 = parts.reshape(width, half)

    parts = summed(contract(lower_10, solved_0, (1, 0)))
    diag_1 = ordered(own_shared[0], got_shared[0], 0)
    parts, diag_1, got_0 = by_deadline(parts, diag_1, from_partner(solved_0))
    whole_0 = ordered(solved_0, got_0, 1)
    pair = ordered(own_shared[1:], got_shared[1:], 1)
    diag_2, diag_3, lower_21, lower_32 = [pair[i] for i in range(4)]
    current = side_1 - parts.sum(0)
    parts = scattered(diag_1, current)
    term_2 = own_term(2) - contract(lower_blocks[1], whole_0, (1, 0))
    parts, got_2 = by_deadline(parts, from_partner(half_of(term_2, row % 2 ^ 1)))
    term_2 = ordered(half_of(term_2, row % 2), got_2, 0)
    term_3 = own_term(3) - contract(lower_blocks[3], whole_0, (1, 0))
    parts = gathered(parts)
    below = below_of(whole_0, 0)
    parts, term_2, term_3, below = by_deadline(parts, term_2, term_3, below)
    solved_1 = parts.reshape(width, half)

    parts = summed(term_2 - contract(lower_21, solved_1, (1, 0)))
    parts, got_1 = by_deadline(parts, from_partner(solved_1))
    whole_1 = ordered(solved_1, got_1, 1)
    parts = scattered(diag_2, parts.sum(0))
    term_3 = term_3 - contract(lower_blocks[4], whole_1, (1, 0))
    parts, got_3 = by_deadline(parts, from_partner(half_of(term_3, row % 2 ^ 1)))
    term_3 = ordered(half_of(term_3, row % 2), got_3, 0)
    parts = gathered(parts)
    below = below + below_of(whole_1, 1)
    parts, below, term_3 = by_deadline(parts, below, term_3)
    solved_2 = parts.reshape(width, half)

    parts = summed(term_3 - contract(lower_32, solved_2, (1, 0)))
    parts, got_2 = by_deadline(parts, from_partner(solved_2))
    parts = scattered(diag_3, parts.sum(0))
    outs = [out_of(whole_0), out_of(whole_1)]
    parts, outs = by_deadline(parts, outs)
    parts = gathered_whole(parts)
    whole_2 = ordered(solved_2, got_2, 1)
    below = below + below_of(whole_2, 2)
    parts, below = by_deadline(parts, below)
    whole_3 = halves_whole(parts)

    below = below + below_of(whole_3, 3)
    shared = swap(below, "col").reshape(col_size, own_width, -1).sum(0)
    shared = shared.reshape(own_width, trail_count, local_rows).transpose(1, 0, 2)
    trail_rest = (own_below - shared).transpose(0, 2, 1)
    return (jnp.stack(outs + [out_of(whole_2), out_of(whole_3)]), trail_rest)


def solution(mesh):
    placed = (
        P(None, "row", None),
        P(None, "col", "row"),
        P(None, "row", "col"),
        P(None, "row", None, "col"),
    )
    return jax.shard_map(
        shards,
        mesh=mesh,
        in_specs=placed,
        out_specs=(P(None, "col", "row"), P(None, "row", "col")),
        check_vma=False,
    )
```

```python
import jax
import jax.numpy as jnp
from jax import lax
from jax.sharding import PartitionSpec as P

PRECISION = lax.Precision.HIGHEST


def contract(left, right, axes):
    return lax.dot_general(
        left,
        right,
        (((axes[0],), (axes[1],)), ((), ())),
        precision=PRECISION,
        preferred_element_type=jnp.float32,
    )


def swap(parts, axis, groups=None):
    return lax.all_to_all(parts, axis, 0, 0, axis_index_groups=groups, tiled=True)


def copies(part, count):
    return jnp.broadcast_to(part[None], (count,) + part.shape)


def by_deadline(*values):
    return lax.optimization_barrier(values)


def shards(right_sides, diag_inverse, lower_blocks, trail_panel):
    step_count = diag_inverse.shape[0]
    trail_count = trail_panel.shape[0]
    local_rows = right_sides.shape[1]
    column_count = right_sides.shape[2]
    width = lower_blocks.shape[2]
    row_size = lax.axis_size("row")
    col_size = lax.axis_size("col")
    members = row_size // 2
    half = column_count // 2
    row = lax.axis_index("row")
    col = lax.axis_index("col")
    even = row % 2 == 0
    row_groups = [[r for r in range(row_size) if r % 2 == g] for g in range(2)]

    def from_partner(value):
        return lax.ppermute(value, "row", [(r, r ^ 1) for r in range(row_size)])

    def ordered(own, got, axis):
        return jnp.concatenate([jnp.where(even, own, got), jnp.where(even, got, own)], axis)

    def half_of(value, which):
        return lax.dynamic_slice_in_dim(value, which * half, half, value.ndim - 1)

    def halves_whole(parts):
        parts = parts.reshape(members, 2, -1, half)
        return parts.transpose(0, 2, 1, 3).reshape(width, column_count)

    def scattered(matrix, current):
        parts = contract(matrix, current, (0, 0)).reshape(members, width // members, half)
        return swap(parts, "row", row_groups)

    def scattered_whole(matrix, current):
        parts = contract(matrix, current, (0, 0))
        return swap(parts.reshape(row_size, width // row_size, column_count), "row")

    def gathered(parts):
        return swap(copies(parts.sum(0), members), "row", row_groups)

    def gathered_whole(parts):
        return swap(copies(parts.sum(0), row_size), "row")

    def summed(update):
        return swap(copies(update, col_size), "col")

    def own_term(block_row):
        return jnp.where(col == 0, right_sides[block_row], 0.0)

    own_diag = diag_inverse.transpose(0, 2, 1)
    trail = [
        trail_panel[:, :, j, :].reshape(trail_count * local_rows, width) for j in range(step_count)
    ]

    def below_of(whole, block_row):
        return contract(whole, trail[block_row], (0, 1))

    own_width = column_count // col_size
    own_below = lax.dynamic_slice_in_dim(
        right_sides[step_count:].transpose(0, 2, 1), col * own_width, own_width, 1
    )

    out_width = column_count // row_size

    def out_of(whole):
        return lax.dynamic_slice_in_dim(whole, row * out_width, out_width, 1)

    parts = scattered_whole(own_diag[0], right_sides[0])
    sent_first = jnp.concatenate([lower_blocks[0], half_of(right_sides[1], row % 2 ^ 1)], 1)
    part = parts.sum(0)
    part = jnp.stack([part[:, :half], part[:, half:]])
    sent = copies(part, members).reshape(row_size, -1, half)
    sent, sent_first = by_deadline(sent, sent_first)
    parts = swap(sent, "row")
    got_first = from_partner(sent_first)
    own_shared = jnp.concatenate([own_diag[1:], lower_blocks[2:3], lower_blocks[5:]])
    got_first, own_shared = by_deadline(got_first, own_shared)
    got_shared = from_partner(own_shared)
    lower_10 = ordered(lower_blocks[0], got_first[:, :width], 0)
    side_1 = ordered(half_of(right_sides[1], row % 2), got_first[:, width:], 0)
    parts, trail, lower_10, side_1 = by_deadline(parts, trail, lower_10, side_1)
    solved_0 = parts.reshape(width, half)

    parts = summed(contract(lower_10, solved_0, (1, 0)))
    diag_1 = ordered(own_shared[0], got_shared[0], 0)
    parts, diag_1, got_0 = by_deadline(parts, diag_1, from_partner(solved_0))
    whole_0 = ordered(solved_0, got_0, 1)
    pair = ordered(own_shared[1:], got_shared[1:], 1)
    diag_2, diag_3, lower_21, lower_32 = [pair[i] for i in range(4)]
    current = side_1 - parts.sum(0)
    parts = scattered(diag_1, current)
    term_2 = own_term(2) - contract(lower_blocks[1], whole_0, (1, 0))
    parts, got_2 = by_deadline(parts, from_partner(half_of(term_2, row % 2 ^ 1)))
    term_2 = ordered(half_of(term_2, row % 2), got_2, 0)
    term_3 = own_term(3) - contract(lower_blocks[3], whole_0, (1, 0))
    parts = gathered(parts)
    below = below_of(whole_0, 0)
    parts, term_2, term_3, below = by_deadline(parts, term_2, term_3, below)
    solved_1 = parts.reshape(width, half)

    parts = summed(term_2 - contract(lower_21, solved_1, (1, 0)))
    parts, got_1 = by_deadline(parts, from_partner(solved_1))
    whole_1 = ordered(solved_1, got_1, 1)
    parts = scattered(diag_2, parts.sum(0))
    term_3 = term_3 - contract(lower_blocks[4], whole_1, (1, 0))
    parts, got_3 = by_deadline(parts, from_partner(half_of(term_3, row % 2 ^ 1)))
    term_3 = ordered(half_of(term_3, row % 2), got_3, 0)
    parts = gathered(parts)
    below = below + below_of(whole_1, 1)
    parts, below, term_3 = by_deadline(parts, below, term_3)
    solved_2 = parts.reshape(width, half)

    parts = summed(term_3 - contract(lower_32, solved_2, (1, 0)))
    parts, got_2 = by_deadline(parts, from_partner(solved_2))
    parts = scattered(diag_3, parts.sum(0))
    outs = [out_of(whole_0), out_of(whole_1)]
    parts, outs = by_deadline(parts, outs)
    parts = gathered_whole(parts)
    whole_2 = ordered(solved_2, got_2, 1)
    below = below + below_of(whole_2, 2)
    parts, below = by_deadline(parts, below)
    whole_3 = halves_whole(parts)

    below = below + below_of(whole_3, 3)
    shared = swap(below, "col").reshape(col_size, own_width, -1).sum(0)
    shared = shared.reshape(own_width, trail_count, local_rows).transpose(1, 0, 2)
    trail_rest = (own_below - shared).transpose(0, 2, 1)
    return (jnp.stack(outs + [out_of(whole_2), out_of(whole_3)]), trail_rest)


def solution(mesh):
    placed = (
        P(None, "row", None),
        P(None, "col", "row"),
        P(None, "row", "col"),
        P(None, "row", None, "col"),
    )
    return jax.shard_map(
        shards,
        mesh=mesh,
        in_specs=placed,
        out_specs=(P(None, "col", "row"), P(None, "row", "col")),
        check_vma=False,
    )
```

```python
import jax
import jax.numpy as jnp
from jax import lax
from jax.sharding import PartitionSpec as P

PRECISION = lax.Precision.HIGHEST


def contract(left, right, axes):
    return lax.dot_general(
        left,
        right,
        (((axes[0],), (axes[1],)), ((), ())),
        precision=PRECISION,
        preferred_element_type=jnp.float32,
    )


def swap(parts, axis, groups=None):
    return lax.all_to_all(parts, axis, 0, 0, axis_index_groups=groups, tiled=True)


def copies(part, count):
    return jnp.broadcast_to(part[None], (count,) + part.shape)


def by_deadline(*values):
    return lax.optimization_barrier(values)


def shards(right_sides, diag_inverse, lower_blocks, trail_panel):
    step_count = diag_inverse.shape[0]
    trail_count = trail_panel.shape[0]
    local_rows = right_sides.shape[1]
    column_count = right_sides.shape[2]
    width = lower_blocks.shape[2]
    row_size = lax.axis_size("row")
    col_size = lax.axis_size("col")
    members = row_size // 2
    half = column_count // 2
    row = lax.axis_index("row")
    col = lax.axis_index("col")
    even = row % 2 == 0
    row_groups = [[r for r in range(row_size) if r % 2 == g] for g in range(2)]

    def from_partner(value):
        return lax.ppermute(value, "row", [(r, r ^ 1) for r in range(row_size)])

    def ordered(own, got, axis):
        return jnp.concatenate([jnp.where(even, own, got), jnp.where(even, got, own)], axis)

    def half_of(value, which):
        return lax.dynamic_slice_in_dim(value, which * half, half, value.ndim - 1)

    def halves_whole(parts):
        parts = parts.reshape(members, 2, -1, half)
        return parts.transpose(0, 2, 1, 3).reshape(width, column_count)

    def scattered(matrix, current):
        parts = contract(matrix, current, (0, 0)).reshape(members, width // members, half)
        return swap(parts, "row", row_groups)

    def scattered_whole(matrix, current):
        parts = contract(matrix, current, (0, 0))
        return swap(parts.reshape(row_size, width // row_size, column_count), "row")

    def gathered(parts):
        return swap(copies(parts.sum(0), members), "row", row_groups)

    def gathered_whole(parts):
        return swap(copies(parts.sum(0), row_size), "row")

    def summed(update):
        return swap(copies(update, col_size), "col")

    def own_term(block_row):
        return jnp.where(col == 0, right_sides[block_row], 0.0)

    own_diag = diag_inverse.transpose(0, 2, 1)
    trail = [
        trail_panel[:, :, j, :].reshape(trail_count * local_rows, width) for j in range(step_count)
    ]

    def below_of(whole, block_row):
        return contract(whole, trail[block_row], (0, 1))

    own_width = column_count // col_size
    own_below = lax.dynamic_slice_in_dim(
        right_sides[step_count:].transpose(0, 2, 1), col * own_width, own_width, 1
    )

    out_width = column_count // row_size

    def out_of(whole):
        return lax.dynamic_slice_in_dim(whole, row * out_width, out_width, 1)

    parts = scattered_whole(own_diag[0], right_sides[0])
    sent_first = jnp.concatenate([lower_blocks[0], half_of(right_sides[1], row % 2 ^ 1)], 1)
    got_first = from_partner(sent_first)
    parts, got_first, trail = by_deadline(parts, got_first, trail)
    part = parts.sum(0)
    part = jnp.stack([part[:, :half], part[:, half:]])
    sent = copies(part, members).reshape(row_size, -1, half)
    parts = swap(sent, "row")
    own_shared = jnp.concatenate([own_diag[1:], lower_blocks[2:3], lower_blocks[5:]])
    got_first, own_shared = by_deadline(got_first, own_shared)
    got_shared = from_partner(own_shared)
    lower_10 = ordered(lower_blocks[0], got_first[:, :width], 0)
    side_1 = ordered(half_of(right_sides[1], row % 2), got_first[:, width:], 0)
    parts, lower_10, side_1 = by_deadline(parts, lower_10, side_1)
    solved_0 = parts.reshape(width, half)

    parts = summed(contract(lower_10, solved_0, (1, 0)))
    diag_1 = ordered(own_shared[0], got_shared[0], 0)
    parts, diag_1, got_0 = by_deadline(parts, diag_1, from_partner(solved_0))
    whole_0 = ordered(solved_0, got_0, 1)
    pair = ordered(own_shared[1:], got_shared[1:], 1)
    diag_2, diag_3, lower_21, lower_32 = [pair[i] for i in range(4)]
    current = side_1 - parts.sum(0)
    parts = scattered(diag_1, current)
    term_2 = own_term(2) - contract(lower_blocks[1], whole_0, (1, 0))
    parts, got_2 = by_deadline(parts, from_partner(half_of(term_2, row % 2 ^ 1)))
    term_2 = ordered(half_of(term_2, row % 2), got_2, 0)
    term_3 = own_term(3) - contract(lower_blocks[3], whole_0, (1, 0))
    parts = gathered(parts)
    below = below_of(whole_0, 0)
    parts, term_2, term_3, below = by_deadline(parts, term_2, term_3, below)
    solved_1 = parts.reshape(width, half)

    parts = summed(term_2 - contract(lower_21, solved_1, (1, 0)))
    parts, got_1 = by_deadline(parts, from_partner(solved_1))
    whole_1 = ordered(solved_1, got_1, 1)
    parts = scattered(diag_2, parts.sum(0))
    term_3 = term_3 - contract(lower_blocks[4], whole_1, (1, 0))
    parts, got_3 = by_deadline(parts, from_partner(half_of(term_3, row % 2 ^ 1)))
    term_3 = ordered(half_of(term_3, row % 2), got_3, 0)
    parts = gathered(parts)
    below = below + below_of(whole_1, 1)
    parts, below, term_3 = by_deadline(parts, below, term_3)
    solved_2 = parts.reshape(width, half)

    parts = summed(term_3 - contract(lower_32, solved_2, (1, 0)))
    parts, got_2 = by_deadline(parts, from_partner(solved_2))
    parts = scattered(diag_3, parts.sum(0))
    outs = [out_of(whole_0), out_of(whole_1)]
    parts, outs = by_deadline(parts, outs)
    parts = gathered_whole(parts)
    whole_2 = ordered(solved_2, got_2, 1)
    below = below + below_of(whole_2, 2)
    parts, below = by_deadline(parts, below)
    whole_3 = halves_whole(parts)

    below = below + below_of(whole_3, 3)
    shared = swap(below, "col").reshape(col_size, own_width, -1).sum(0)
    shared = shared.reshape(own_width, trail_count, local_rows).transpose(1, 0, 2)
    trail_rest = (own_below - shared).transpose(0, 2, 1)
    return (jnp.stack(outs + [out_of(whole_2), out_of(whole_3)]), trail_rest)


def solution(mesh):
    placed = (
        P(None, "row", None),
        P(None, "col", "row"),
        P(None, "row", "col"),
        P(None, "row", None, "col"),
    )
    return jax.shard_map(
        shards,
        mesh=mesh,
        in_specs=placed,
        out_specs=(P(None, "col", "row"), P(None, "row", "col")),
        check_vma=False,
    )
```
